32 devices in a mesh: dp: 4 (over z), expert: 4 (over x, core), tensor: 2 (over y).
Axes of the slice: x: 2, y: 2, z: 4, core: 2. Of those that a mesh axis runs over, the one named last changes fastest.
Arguments:
- tokens: bfloat16 [2048, 2048], P(('dp', 'expert')), may hold values from -6 to 6
- cotangent: bfloat16 [2048, 2048], P(('dp', 'expert')), may hold values from -6 to 6
- scores: float32 [2048, 8], P(('dp', 'expert')), may hold values from 0.05 to 1
- routes: int32 [2048, 1], P(('dp', 'expert')), may hold values from 0 to 7; in each aligned block of 128 rows (0 to 127, 128 to 255, ...) at most 32 rows name the same one
- w_gate: bfloat16 [8, 2048, 768], P('expert', 'dp', 'tensor'), may hold values from -0.125 to 0.125
- w_up: bfloat16 [8, 2048, 768], P('expert', 'dp', 'tensor'), may hold values from -0.125 to 0.125
- w_down: bfloat16 [8, 768, 2048], P('expert', 'tensor', 'dp'), may hold values from -0.21875 to 0.21875
Outputs:
- output: bfloat16 [2048, 2048], P(('dp', 'expert'), 'tensor')
- grad_tokens: bfloat16 [2048, 2048], P(('dp', 'expert'), 'tensor')
- grad_gate: float32 [8, 2048, 768], P('expert', 'dp', 'tensor')
- grad_up: float32 [8, 2048, 768], P('expert', 'dp', 'tensor')
- grad_down: float32 [8, 768, 2048], P('expert', 'tensor', 'dp')
The draws below stay inside these ranges and needn't reach their ends.
Inputs may be any that keep to these rules, and one draw needn't show every extreme that they name: `routes`: each row names 1 different experts. Among the rows of one token block no expert is named more than 32 times, and 32 is reached.
All inputs are finite; a program needn't handle non-finite values.
Results may differ from the reference program's by a relative error of at most 0.019.
Values may be sent and summed in bfloat16 or wider, within the bound.
No kernel may reach another device: no remote copies, remote signals or barrier semaphores. Data moves between devices by JAX's collectives and lax.ppermute only.
A program may use at most 64 MiB of HBM per device.

```python
import math
import jax
import jax.numpy as jnp
import numpy as np
from jax import lax

D = 2048
FF = 768
TOP = 8
FLIGHT = 1
TOK_DEV = 128
EXPERTS = 8
TOKEN_GROUPS = 4
SOURCES = 4
UNIT_GROUPS = 2
SHARE = 384
CAP = 32
TOKENS = 2048


def steps_of(key, shape, split, low, high):
    level = 1.0
    for dim, parts in split:
        heights = jax.random.uniform(jax.random.fold_in(jax.random.fold_in(key, 6), dim), (parts,), jnp.float32, low / len(split), high / len(split))
        level = level * jnp.repeat(jnp.exp(heights), shape[dim] // parts).reshape((-1,) + (1,) * (len(shape) - 1 - dim))
    return level


def deal_out(rng, own, number, rows, amount, top, most, lean):
    sequence = jax.random.permutation(rng, amount)
    heavy_load, usual = portions_of(amount, rows * top, most, lean, True), portions_of(amount, rows * top, most, lean, False)
    places = jnp.arange(amount)

    def named(lengths, rotation):
        used = int((lengths > 0).sum())
        fixed = max(1, used // 4)
        moved = fixed + (places - fixed + rotation * (used - fixed)) % max(1, amount - fixed)
        return jnp.zeros((amount,), jnp.int32).at[sequence[jnp.where(places < fixed, places, moved)]].set(jnp.asarray(lengths, jnp.int32))

    lengths = jnp.where(number % 4 == 0, named(heavy_load, number // 4), named(usual, number - number // 4 - 1))
    mixed = jax.random.permutation(jax.random.fold_in(own, 3), amount)
    giver, taker = mixed[0:amount // 2 * 2:2], mixed[1:amount // 2 * 2:2]
    room = jnp.minimum(lengths[giver] - 1, most - lengths[taker]) // 2
    room = jnp.where((giver == sequence[0]) | (taker == sequence[0]) | (lengths[taker] == 0), 0, jnp.maximum(room, 0))
    moved = jax.random.randint(jax.random.fold_in(own, 4), (amount // 2,), 0, 1 << 20) % (room + 1)
    lengths = lengths.at[giver].add(-moved).at[taker].add(moved)
    members = jnp.searchsorted(jnp.cumsum(lengths), jnp.arange(rows * top), side="right").astype(jnp.int32)
    grid = members.reshape(top, rows).T
    grid = grid[jax.random.permutation(jax.random.fold_in(own, 1), rows)]
    rotation = jax.random.randint(jax.random.fold_in(own, 2), (rows, 1), 0, top)
    return jnp.take_along_axis(grid, (jnp.arange(top)[None, :] + rotation) % top, axis=1)


def portions_of(amount, total, bound, skew, full):
    weights = [(1 << 20) // math.isqrt(standing ** skew) + 1 for standing in range(1, amount + 1)]
    largest = bound if full else min(bound, max(-(-total // amount), total * weights[0] // sum(weights)))
    least = 1 if total - largest >= amount - 1 else 0
    counts, spare = [largest] + [least] * (amount - 1), total - largest - least * (amount - 1)
    while spare > 0:
        candidates = [i for i in range(1, amount) if counts[i] < largest] or [i for i in range(1, amount) if counts[i] < bound]
        mass, remaining = sum([weights[i] for i in candidates]), spare
        for i in candidates:
            more = min(bound - counts[i], max(1, remaining * weights[i] // mass), spare)
            counts[i] = counts[i] + more
            spare = spare - more
    return np.array(counts)


def noise(rng, shape, scale, limit, split=(), kind=jnp.bfloat16):
    array = scale * jax.random.normal(rng, shape, jnp.float32)
    if split:
        array = array * steps_of(rng, shape, split, -0.22, 0.18)
    return jnp.clip(array, -limit, limit).astype(kind)


def setup_inputs(seed: int = 0) -> dict:
    keys = jax.random.split(jax.random.key(seed), 8)
    tokens = noise(keys[0], (TOKENS, D), 1.0, 6.0, ((0, 16),))
    cotangent = noise(keys[1], (TOKENS, D), 1.0, 6.0, ((0, 16),))
    scores = jnp.clip(jnp.exp(math.log(1.0) - 2.9957323 * jax.random.uniform(keys[2], (TOKENS, TOP), jnp.float32) ** steps_of(keys[2], (TOKENS, TOP), ((0, 16),), -0.2, 0.2)), 0.05, 1.0)
    routes_keys = jax.random.split(jax.random.fold_in(keys[3], 1), TOKENS // TOK_DEV)
    routes_turns = jax.random.permutation(jax.random.fold_in(keys[3], 3), TOKENS // TOK_DEV)
    routes = jax.vmap(lambda own, number: deal_out(jax.random.fold_in(keys[3], 2), own, number, TOK_DEV, EXPERTS, FLIGHT, CAP, 2))(routes_keys, routes_turns).reshape((TOKENS, FLIGHT))
    w_gate = noise(keys[4], (EXPERTS, D, FF), D ** -0.5, 0.125, ((0, 4), (1, 4), (2, 2)))
    w_up = noise(keys[5], (EXPERTS, D, FF), D ** -0.5, 0.125, ((0, 4), (1, 4), (2, 2)))
    w_down = noise(keys[6], (EXPERTS, FF, D), FF ** -0.5, 0.21875, ((0, 4), (1, 2), (2, 4)))
    return dict(tokens=tokens, cotangent=cotangent, scores=scores, routes=routes, w_gate=w_gate, w_up=w_up, w_down=w_down)


def rounded(value):
    return lax.optimization_barrier(value.astype(jnp.bfloat16)).astype(jnp.float32)


def slot_onehot(route_block, expert_count, capacity):
    flat = route_block.reshape(-1).astype(jnp.int32)
    member = (flat[:, None] == jnp.arange(expert_count, dtype=jnp.int32)[None, :]).astype(jnp.int32)
    before = jnp.cumsum(member, axis=0) - member
    place = jnp.sum(before * member, axis=1)
    slot_ids = flat * capacity + place
    return slot_ids[:, None] == jnp.arange(expert_count * capacity, dtype=jnp.int32)[None, :]


def reference(tokens, cotangent, scores, routes, w_gate, w_up, w_down):
    highest = lax.Precision.HIGHEST
    owners = SOURCES
    slots = EXPERTS * CAP
    gate_full = w_gate.astype(jnp.float32)
    up_full = w_up.astype(jnp.float32)
    down_full = w_down.astype(jnp.float32)
    sum_gate = jnp.zeros((EXPERTS, D, FF), jnp.float32)
    sum_up = jnp.zeros((EXPERTS, D, FF), jnp.float32)
    sum_down = jnp.zeros((EXPERTS, FF, D), jnp.float32)
    outs_y = []
    outs_x = []
    span = owners * TOK_DEV
    for group in range(TOKEN_GROUPS):
        rows_in = tokens[group * span:(group + 1) * span].reshape(owners, TOK_DEV, D)
        rows_cot = cotangent[group * span:(group + 1) * span].reshape(owners, TOK_DEV, D)
        block_scores = scores[group * span:(group + 1) * span].reshape(owners, TOK_DEV, TOP)
        block_routes = routes[group * span:(group + 1) * span].reshape(owners, TOK_DEV, FLIGHT)
        table = jax.vmap(lambda one: slot_onehot(one, EXPERTS, CAP))(block_routes).astype(jnp.float32)
        mix = (block_scores / jnp.sum(block_scores, axis=2, keepdims=True))[:, :, :FLIGHT]
        rep_x = jnp.repeat(rows_in.astype(jnp.float32), FLIGHT, axis=1)
        rep_d = rounded(mix[:, :, :, None] * rows_cot.astype(jnp.float32)[:, :, None, :]).reshape(owners, TOK_DEV * FLIGHT, D)
        send_x = jnp.einsum('nrs,nrd->nsd', table, rep_x, precision=highest)
        send_d = jnp.einsum('nrs,nrd->nsd', table, rep_d, precision=highest)
        x_rows = send_x.reshape(owners, EXPERTS, CAP, D).transpose(1, 0, 2, 3).reshape(EXPERTS, owners * CAP, D)
        d_rows = send_d.reshape(owners, EXPERTS, CAP, D).transpose(1, 0, 2, 3).reshape(EXPERTS, owners * CAP, D)
        gate_act = jnp.einsum('erd,edf->erf', x_rows, gate_full, precision=highest)
        up_act = jnp.einsum('erd,edf->erf', x_rows, up_full, precision=highest)
        sigma = jax.nn.sigmoid(gate_act)
        silu_act = gate_act * sigma
        hidden = rounded(silu_act * up_act)
        back_grad = jnp.einsum('erd,efd->erf', d_rows, down_full, precision=highest)
        grad_act_gate = rounded(back_grad * up_act * sigma * (1.0 + gate_act * (1.0 - sigma)))
        grad_act_up = rounded(back_grad * silu_act)
        out_rows = jnp.zeros((EXPERTS, owners * CAP, D), jnp.float32)
        in_rows = jnp.zeros((EXPERTS, owners * CAP, D), jnp.float32)
        for unit in range(UNIT_GROUPS):
            lo = unit * SHARE
            hi = lo + SHARE
            out_rows = out_rows + rounded(jnp.einsum('erf,efd->erd', hidden[:, :, lo:hi], down_full[:, lo:hi, :], precision=highest))
            in_term = jnp.einsum('erf,edf->erd', grad_act_gate[:, :, lo:hi], gate_full[:, :, lo:hi], precision=highest)
            in_term = in_term + jnp.einsum('erf,edf->erd', grad_act_up[:, :, lo:hi], up_full[:, :, lo:hi], precision=highest)
            in_rows = in_rows + rounded(in_term)
        back_y = out_rows.reshape(EXPERTS, owners, CAP, D).transpose(1, 0, 2, 3).reshape(owners, slots, D)
        back_x = in_rows.reshape(EXPERTS, owners, CAP, D).transpose(1, 0, 2, 3).reshape(owners, slots, D)
        spread = table.reshape(owners, TOK_DEV, FLIGHT, slots)
        weighted = jnp.einsum('ntks,ntk->nts', spread, mix, precision=highest)
        plain = jnp.sum(spread, axis=2)
        outs_y.append(jnp.einsum('nts,nsd->ntd', weighted, back_y, precision=highest))
        outs_x.append(jnp.einsum('nts,nsd->ntd', plain, back_x, precision=highest))
        sum_gate = sum_gate + rounded(jnp.einsum('erd,erf->edf', x_rows, grad_act_gate, precision=highest))
        sum_up = sum_up + rounded(jnp.einsum('erd,erf->edf', x_rows, grad_act_up, precision=highest))
        sum_down = sum_down + rounded(jnp.einsum('erf,erd->efd', hidden, d_rows, precision=highest))
    output = jnp.concatenate(outs_y, axis=0).reshape(TOKENS, D).astype(jnp.bfloat16)
    grad_tokens = jnp.concatenate(outs_x, axis=0).reshape(TOKENS, D).astype(jnp.bfloat16)
    return output, grad_tokens, sum_gate, sum_up, sum_down
```

```python
import jax
import jax.numpy as jnp
from jax import lax
from jax.sharding import PartitionSpec as P

F32 = jnp.float32
BF16 = jnp.bfloat16


def slots_of(route_block, expert_count, capacity):
    flat = route_block.reshape(-1)
    member = (flat[:, None] == jnp.arange(expert_count, dtype=jnp.int32)[None, :]).astype(jnp.int32)
    before = jnp.cumsum(member, axis=0) - member
    place = jnp.sum(before * member, axis=1)
    return flat * capacity + place


def on_device(tokens, cotangent, scores, routes, w_gate, w_up, w_down):
    tok_count = tokens.shape[0]
    owners = lax.axis_size("expert")
    local_count = w_gate.shape[0]
    expert_count = local_count * owners
    capacity = min(tok_count, 2 * tok_count // expert_count)
    slot_total = expert_count * capacity
    slot_ids = slots_of(routes, expert_count, capacity)
    groups_slots = lax.all_gather(slot_ids, "dp", axis=0, tiled=False)
    mix = scores[:, :1] / jnp.sum(scores, axis=1, keepdims=True)
    x_chunk = lax.all_to_all(tokens, "dp", split_axis=1, concat_axis=0, tiled=True)
    weighted = (mix * cotangent.astype(F32)).astype(BF16)
    d_chunk = lax.all_to_all(weighted, "dp", split_axis=1, concat_axis=0, tiled=True)
    groups = groups_slots.shape[0]
    width = x_chunk.shape[1]
    picker = (
        groups_slots[:, None, :] == jnp.arange(slot_total, dtype=jnp.int32)[None, :, None]
    ).astype(BF16)
    pick_send = picker.reshape(groups, owners, local_count * capacity, tok_count)

    def dispatch(chunk):
        rows = chunk.reshape(groups, tok_count, width)
        send = jnp.einsum("gesr,grk->egsk", pick_send, rows, preferred_element_type=F32).astype(BF16)
        got = lax.all_to_all(send, "expert", split_axis=0, concat_axis=0, tiled=True)
        return got.reshape(owners, groups, local_count, capacity, width)

    rows_x = dispatch(x_chunk)
    rows_d = dispatch(d_chunk)

    def scattered(partial):
        return lax.psum_scatter(
            partial.astype(BF16).reshape(-1, partial.shape[4]), "dp", scatter_dimension=0, tiled=True
        ).astype(F32)

    gate_act = scattered(
        jnp.einsum("sgick,ikf->giscf", rows_x, w_gate, preferred_element_type=F32)
    )
    up_act = scattered(jnp.einsum("sgick,ikf->giscf", rows_x, w_up, preferred_element_type=F32))
    back_grad = scattered(
        jnp.einsum("sgick,ifk->giscf", rows_d, w_down, preferred_element_type=F32)
    )
    sigma = jax.nn.sigmoid(gate_act)
    silu_act = gate_act * sigma
    hidden = (silu_act * up_act).astype(BF16)
    grad_act_gate = (back_grad * up_act * sigma * (1.0 + gate_act * (1.0 - sigma))).astype(BF16)
    grad_act_up = (back_grad * silu_act).astype(BF16)

    def gathered(act):
        whole = lax.all_gather(act, "dp", axis=0, tiled=True)
        return whole.reshape(groups, local_count, owners, capacity, act.shape[1])

    hidden = gathered(hidden)
    grad_act_gate = gathered(grad_act_gate)
    grad_act_up = gathered(grad_act_up)
    part_out = jnp.einsum("giscf,ifk->sgick", hidden, w_down, preferred_element_type=F32)
    part_in = jnp.einsum("giscf,ikf->sgick", grad_act_gate, w_gate, preferred_element_type=F32)
    part_in = part_in + jnp.einsum(
        "giscf,ikf->sgick", grad_act_up, w_up, preferred_element_type=F32
    )

    pick_back = picker.reshape(groups, owners, local_count, capacity, tok_count)

    def combine(part):
        back = lax.all_to_all(part.astype(BF16), "expert", split_axis=0, concat_axis=0, tiled=True)
        rows = jnp.einsum("geicr,egick->grk", pick_back, back, preferred_element_type=F32)
        whole = lax.all_to_all(rows.astype(BF16), "dp", split_axis=0, concat_axis=2, tiled=True)
        whole = whole.reshape(tok_count, groups * width)
        return lax.psum_scatter(whole, "tensor", scatter_dimension=1, tiled=True).astype(F32)

    output = (mix * combine(part_out)).astype(BF16)
    grad_tokens = combine(part_in).astype(BF16)
    grad_gate = jnp.einsum("sgick,giscf->ikf", rows_x, grad_act_gate, preferred_element_type=F32)
    grad_up = jnp.einsum("sgick,giscf->ikf", rows_x, grad_act_up, preferred_element_type=F32)
    grad_down = jnp.einsum("giscf,sgick->ifk", hidden, rows_d, preferred_element_type=F32)
    return (output, grad_tokens, grad_gate, grad_up, grad_down)


def solution(mesh):
    in_specs = (
        P(("dp", "expert"), None),
        P(("dp", "expert"), None),
        P(("dp", "expert"), None),
        P(("dp", "expert"), None),
        P("expert", "dp", "tensor"),
        P("expert", "dp", "tensor"),
        P("expert", "tensor", "dp"),
    )
    out_specs = (
        P(("dp", "expert"), "tensor"),
        P(("dp", "expert"), "tensor"),
        P("expert", "dp", "tensor"),
        P("expert", "dp", "tensor"),
        P("expert", "tensor", "dp"),
    )
    return jax.shard_map(
        on_device, mesh=mesh, in_specs=in_specs, out_specs=out_specs, check_vma=False
    )
```

```python
import jax
import jax.numpy as jnp
from jax import lax
from jax.sharding import PartitionSpec as P

F32 = jnp.float32
BF16 = jnp.bfloat16


def dot(eq, a, b):
    return jnp.einsum(eq, a, b, preferred_element_type=F32)


def on_device(tokens, cotangent, scores, routes, w_gate, w_up, w_down):
    tok_count, model_width = tokens.shape
    owners = lax.axis_size("expert")
    groups = lax.axis_size("dp")
    sharers = lax.axis_size("tensor")
    local_count = w_gate.shape[0]
    expert_count = local_count * owners
    capacity = min(tok_count, 2 * tok_count // expert_count)
    held = local_count * capacity
    width = model_width // groups
    my_group = lax.axis_index("dp")
    my_owner = lax.axis_index("expert")
    my_part = lax.axis_index("tensor")

    def shift(value, step):
        if step % groups == 0:
            return value
        return lax.ppermute(value, "dp", [(j, (j + step) % groups) for j in range(groups)])

    def swap(value, bits):
        if bits == 0:
            return value
        return lax.ppermute(value, "expert", [(j, j ^ bits) for j in range(owners)])

    def chunks_out(rows):
        parts = []
        for step in range(groups):
            start = lax.rem(my_group + step, groups) * width
            parts.append(shift(lax.dynamic_slice(rows, (0, start), (tok_count, width)), step))
        return parts

    def picked(stack, index):
        return lax.dynamic_index_in_dim(stack, lax.rem(index + groups, groups), 0, keepdims=False)

    def by_group(parts):
        stack = jnp.stack(parts)
        return jnp.stack([picked(stack, my_group - g) for g in range(groups)])

    routes_all = by_group([shift(routes[:, 0], step) for step in range(groups)])
    x_chunk = by_group(chunks_out(tokens))
    mix = scores[:, :1] / jnp.sum(scores, axis=1, keepdims=True)
    weighted = (mix * cotangent.astype(F32)).astype(BF16)
    d_chunk = by_group(chunks_out(weighted))

    member = (routes_all[:, :, None] == jnp.arange(expert_count, dtype=jnp.int32)).astype(F32)
    earlier = jnp.tril(jnp.ones((tok_count, tok_count), BF16), -1)
    before = dot("ab,gbe->gae", earlier, member.astype(BF16))
    place = jnp.sum(before * member, axis=2).astype(jnp.int32)
    slot_ids = routes_all * capacity + place

    def picker(bits):
        base = (my_owner ^ bits) * held
        wanted = base + jnp.arange(held, dtype=jnp.int32).reshape(local_count, 1, capacity, 1)
        return (slot_ids[None, :, None, :] == wanted).astype(BF16)

    pickers = [picker(bits) for bits in range(owners)]

    def dispatch(chunk):
        got = []
        for bits in range(owners):
            send = dot("igct,gtk->igck", pickers[bits], chunk).astype(BF16)
            got.append(swap(send.reshape(local_count, groups * capacity, width), bits))
        return [jnp.concatenate([g[i] for g in got], axis=0) for i in range(local_count)]

    rows_x = dispatch(x_chunk)
    rows_d = dispatch(d_chunk)

    def line_sum(part):
        part = part.astype(BF16)
        if groups != 4:
            return lax.psum(part, "dp").astype(F32)
        near = lax.ppermute(part, "dp", [(0, 1), (3, 2)])
        pair = part.astype(F32) + near.astype(F32)
        far = lax.ppermute(pair.astype(BF16), "dp", [(1, 2), (2, 1)])
        total = (pair + far.astype(F32)).astype(BF16)
        back = lax.ppermute(total, "dp", [(1, 0), (2, 3)])
        at_end = (my_group == 0) | (my_group == groups - 1)
        return jnp.where(at_end, back, total).astype(F32)

    experts = range(local_count)
    gate_act, up_act, back_grad = {}, {}, {}
    for i in experts:
        gate_act[i] = line_sum(dot("rk,kf->rf", rows_x[i], w_gate[i]))
        up_act[i] = line_sum(dot("rk,kf->rf", rows_x[i], w_up[i]))
    for i in experts:
        back_grad[i] = line_sum(dot("rk,fk->rf", rows_d[i], w_down[i]))

    part_out, part_in, grad_gate, grad_up, grad_down = [], [], [], [], []
    for i in experts:
        sigma = jax.nn.sigmoid(gate_act[i])
        silu_act = gate_act[i] * sigma
        hidden = (silu_act * up_act[i]).astype(BF16)
        act_gate = (
            back_grad[i] * up_act[i] * sigma * (1.0 + gate_act[i] * (1.0 - sigma))
        ).astype(BF16)
        act_up = (back_grad[i] * silu_act).astype(BF16)
        part_out.append(dot("rf,fk->rk", hidden, w_down[i]).astype(BF16))
        into = dot("rf,kf->rk", act_gate, w_gate[i]) + dot("rf,kf->rk", act_up, w_up[i])
        part_in.append(into.astype(BF16))
        grad_gate.append(dot("rk,rf->kf", rows_x[i], act_gate))
        grad_up.append(dot("rk,rf->kf", rows_x[i], act_up))
        grad_down.append(dot("rf,rk->fk", hidden, rows_d[i]))

    pick_all = jnp.stack(pickers)

    def combine(parts):
        rows = jnp.stack(parts).reshape(local_count, owners, groups, capacity, width)
        back = jnp.stack([swap(rows[:, bits], bits) for bits in range(owners)])
        sums = dot("bigct,bigck->gtk", pick_all, back).astype(BF16)
        mine = jnp.stack(
            [shift(picked(sums, my_group - step), -step) for step in range(groups)]
        )
        whole = jnp.concatenate([picked(mine, c - my_group) for c in range(groups)], axis=1)
        if sharers != 2:
            return lax.psum_scatter(whole, "tensor", scatter_dimension=1, tiled=True).astype(F32)
        half = model_width // 2
        give = lax.dynamic_slice(whole, (0, (1 - my_part) * half), (tok_count, half))
        keep = lax.dynamic_slice(whole, (0, my_part * half), (tok_count, half))
        return keep.astype(F32) + lax.ppermute(give, "tensor", [(0, 1), (1, 0)]).astype(F32)

    output = (mix * combine(part_out)).astype(BF16)
    grad_tokens = combine(part_in).astype(BF16)
    return (output, grad_tokens, jnp.stack(grad_gate), jnp.stack(grad_up), jnp.stack(grad_down))


def solution(mesh):
    in_specs = (
        P(("dp", "expert"), None),
        P(("dp", "expert"), None),
        P(("dp", "expert"), None),
        P(("dp", "expert"), None),
        P("expert", "dp", "tensor"),
        P("expert", "dp", "tensor"),
        P("expert", "tensor", "dp"),
    )
    out_specs = (
        P(("dp", "expert"), "tensor"),
        P(("dp", "expert"), "tensor"),
        P("expert", "dp", "tensor"),
        P("expert", "dp", "tensor"),
        P("expert", "tensor", "dp"),
    )
    return jax.shard_map(
        on_device, mesh=mesh, in_specs=in_specs, out_specs=out_specs, check_vma=False
    )
```

```python
import jax
import jax.numpy as jnp
from jax import lax
from jax.experimental import pallas as pl
from jax.experimental.pallas import tpu as pltpu
from jax.sharding import PartitionSpec as P

F32 = jnp.float32
BF16 = jnp.bfloat16


def dot(eq, a, b):
    return jnp.einsum(eq, a, b, preferred_element_type=F32)


def plain_form(tokens, cotangent, scores, routes, w_gate, w_up, w_down):
    tok_count, model_width = tokens.shape
    owners = lax.axis_size("expert")
    groups = lax.axis_size("dp")
    sharers = lax.axis_size("tensor")
    local_count = w_gate.shape[0]
    expert_count = local_count * owners
    capacity = min(tok_count, 2 * tok_count // expert_count)
    held = local_count * capacity
    width = model_width // groups
    my_group = lax.axis_index("dp")
    my_owner = lax.axis_index("expert")
    my_part = lax.axis_index("tensor")

    def shift(value, step):
        if step % groups == 0:
            return value
        return lax.ppermute(value, "dp", [(j, (j + step) % groups) for j in range(groups)])

    def swap(value, bits):
        if bits == 0:
            return value
        return lax.ppermute(value, "expert", [(j, j ^ bits) for j in range(owners)])

    def chunks_out(rows):
        parts = []
        for step in range(groups):
            start = lax.rem(my_group + step, groups) * width
            parts.append(shift(lax.dynamic_slice(rows, (0, start), (tok_count, width)), step))
        return parts

    def picked(stack, index):
        return lax.dynamic_index_in_dim(stack, lax.rem(index + groups, groups), 0, keepdims=False)

    def by_group(parts):
        stack = jnp.stack(parts)
        return jnp.stack([picked(stack, my_group - g) for g in range(groups)])

    routes_all = by_group([shift(routes[:, 0], step) for step in range(groups)])
    x_chunk = by_group(chunks_out(tokens))
    mix = scores[:, :1] / jnp.sum(scores, axis=1, keepdims=True)
    weighted = (mix * cotangent.astype(F32)).astype(BF16)
    d_chunk = by_group(chunks_out(weighted))

    member = (routes_all[:, :, None] == jnp.arange(expert_count, dtype=jnp.int32)).astype(F32)
    earlier = jnp.tril(jnp.ones((tok_count, tok_count), BF16), -1)
    before = dot("ab,gbe->gae", earlier, member.astype(BF16))
    place = jnp.sum(before * member, axis=2).astype(jnp.int32)
    slot_ids = routes_all * capacity + place

    def picker(bits):
        base = (my_owner ^ bits) * held
        wanted = base + jnp.arange(held, dtype=jnp.int32).reshape(local_count, 1, capacity, 1)
        return (slot_ids[None, :, None, :] == wanted).astype(BF16)

    pickers = [picker(bits) for bits in range(owners)]

    def dispatch(chunk):
        got = []
        for bits in range(owners):
            send = dot("igct,gtk->igck", pickers[bits], chunk).astype(BF16)
            got.append(swap(send.reshape(local_count, groups * capacity, width), bits))
        return [jnp.concatenate([g[i] for g in got], axis=0) for i in range(local_count)]

    rows_x = dispatch(x_chunk)
    rows_d = dispatch(d_chunk)

    def line_sum(part):
        part = part.astype(BF16)
        if groups != 4:
            return lax.psum(part, "dp").astype(F32)
        near = lax.ppermute(part, "dp", [(0, 1), (3, 2)])
        pair = part.astype(F32) + near.astype(F32)
        far = lax.ppermute(pair.astype(BF16), "dp", [(1, 2), (2, 1)])
        total = (pair + far.astype(F32)).astype(BF16)
        back = lax.ppermute(total, "dp", [(1, 0), (2, 3)])
        at_end = (my_group == 0) | (my_group == groups - 1)
        return jnp.where(at_end, back, total).astype(F32)

    experts = range(local_count)
    gate_act, up_act, back_grad = {}, {}, {}
    for i in experts:
        gate_act[i] = line_sum(dot("rk,kf->rf", rows_x[i], w_gate[i]))
        up_act[i] = line_sum(dot("rk,kf->rf", rows_x[i], w_up[i]))
    for i in experts:
        back_grad[i] = line_sum(dot("rk,fk->rf", rows_d[i], w_down[i]))

    part_out, part_in, grad_gate, grad_up, grad_down = [], [], [], [], []
    for i in experts:
        sigma = jax.nn.sigmoid(gate_act[i])
        silu_act = gate_act[i] * sigma
        hidden = (silu_act * up_act[i]).astype(BF16)
        act_gate = (
            back_grad[i] * up_act[i] * sigma * (1.0 + gate_act[i] * (1.0 - sigma))
        ).astype(BF16)
        act_up = (back_grad[i] * silu_act).astype(BF16)
        part_out.append(dot("rf,fk->rk", hidden, w_down[i]).astype(BF16))
        into = dot("rf,kf->rk", act_gate, w_gate[i]) + dot("rf,kf->rk", act_up, w_up[i])
        part_in.append(into.astype(BF16))
        grad_gate.append(dot("rk,rf->kf", rows_x[i], act_gate))
        grad_up.append(dot("rk,rf->kf", rows_x[i], act_up))
        grad_down.append(dot("rf,rk->fk", hidden, rows_d[i]))

    pick_all = jnp.stack(pickers)

    def combine(parts):
        rows = jnp.stack(parts).reshape(local_count, owners, groups, capacity, width)
        back = jnp.stack([swap(rows[:, bits], bits) for bits in range(owners)])
        sums = dot("bigct,bigck->gtk", pick_all, back).astype(BF16)
        mine = jnp.stack(
            [shift(picked(sums, my_group - step), -step) for step in range(groups)]
        )
        whole = jnp.concatenate([picked(mine, c - my_group) for c in range(groups)], axis=1)
        if sharers != 2:
            return lax.psum_scatter(whole, "tensor", scatter_dimension=1, tiled=True).astype(F32)
        half = model_width // 2
        give = lax.dynamic_slice(whole, (0, (1 - my_part) * half), (tok_count, half))
        keep = lax.dynamic_slice(whole, (0, my_part * half), (tok_count, half))
        return keep.astype(F32) + lax.ppermute(give, "tensor", [(0, 1), (1, 0)]).astype(F32)

    output = (mix * combine(part_out)).astype(BF16)
    grad_tokens = combine(part_in).astype(BF16)
    return (output, grad_tokens, jnp.stack(grad_gate), jnp.stack(grad_up), jnp.stack(grad_down))


VMEM_LIMIT = 48 * 1024 * 1024


def call(body, outs, ins, scratch=(), flops=0, specs=None):
    moved = sum(a.size * a.dtype.itemsize for a in ins)
    moved += sum(o.size * o.dtype.itemsize for o in outs)
    many = pl.BlockSpec(memory_space=pltpu.VMEM)
    return pl.pallas_call(
        body,
        out_shape=outs,
        grid=() if specs is None else (1,),
        in_specs=[many] * len(ins) if specs is None else specs,
        out_specs=[many] * len(outs),
        scratch_shapes=list(scratch),
        compiler_params=pltpu.CompilerParams(vmem_limit_bytes=VMEM_LIMIT),
        cost_estimate=pl.CostEstimate(flops=flops, bytes_accessed=moved, transcendentals=0),
    )(*ins)


def arr(shape, dtype=BF16):
    return jax.ShapeDtypeStruct(shape, dtype)


def mm(a, b):
    return jnp.dot(a, b, preferred_element_type=F32)


def mm_nt(a, b):
    return lax.dot_general(a, b, (((1,), (1,)), ((), ())), preferred_element_type=F32)


def mm_tn(a, b):
    return lax.dot_general(a, b, (((0,), (0,)), ((), ())), preferred_element_type=F32)


def kernel_form(tokens, cotangent, scores, routes, w_gate, w_up, w_down):
    toks, model_width = tokens.shape
    owners, groups = lax.axis_size("expert"), lax.axis_size("dp")
    local, width, units = w_gate.shape
    expert_count = local * owners
    cap = min(toks, 2 * toks // expert_count)
    held = local * cap
    slot_total = expert_count * cap
    pair_rows = groups // 2 * cap
    half_rows = local * owners * pair_rows
    block = owners * pair_rows
    extra = 16

    def shift(value, step):
        return lax.ppermute(value, "dp", [(j, (j + step) % groups) for j in range(groups)])

    def swap(value, bits):
        return lax.ppermute(value, "expert", [(j, j ^ bits) for j in range(owners)])

    def near_hop(value):
        return lax.ppermute(value, "dp", [(0, 1), (3, 2)])

    def far_hop(value):
        return lax.ppermute(value, "dp", [(1, 2), (2, 1)])

    def back_hop(value):
        return lax.ppermute(value, "dp", [(1, 0), (2, 3)])

    def group_at(step):
        return lax.rem(lax.axis_index("dp") + step + groups, groups)

    def columns_at(step):
        return pl.ds(pl.multiple_of(group_at(step) * width, width), width)

    def pack_body(tok_ref, route_ref, *out_refs):
        row = lax.broadcasted_iota(jnp.int32, (extra, toks), 0)
        line = jnp.broadcast_to(route_ref[...].astype(F32), (extra, toks))
        line = jnp.where(row == 0, line, 0.0).astype(BF16)
        for step in range(groups):
            out = out_refs[step]
            out[0:toks, :] = tok_ref[:, columns_at(step)]
            out[toks : toks + extra, :] = jnp.zeros((extra, width), BF16)
            out[toks : toks + extra, 0:toks] = line

    x_pack = call(
        pack_body, [arr((toks + extra, width))] * groups, [tokens, routes.reshape(1, toks)]
    )
    x_got = [x_pack[0]] + [shift(x_pack[step], step) for step in range(1, groups)]

    def slots_row(line):
        first = lax.broadcasted_iota(jnp.int32, (toks, toks), 0)
        second = lax.broadcasted_iota(jnp.int32, (toks, toks), 1)
        whole = jnp.broadcast_to(line, (toks, toks))
        column = jnp.sum(jnp.where(first == second, whole, 0.0), axis=1, keepdims=True)
        same = (column == whole) & (first < second)
        place = jnp.sum(jnp.where(same, 1.0, 0.0), axis=0, keepdims=True)
        slot = (line * float(cap) + place).astype(jnp.int32)
        return slot ^ (lax.axis_index("expert") * held)

    def picker(slot):
        row = lax.broadcasted_iota(jnp.int32, (slot_total, toks), 0)
        return jnp.where(row == jnp.broadcast_to(slot, (slot_total, toks)), 1.0, 0.0).astype(BF16)

    def send_rows(pick, rows, group, out_refs):
        sent = mm(pick, rows).astype(BF16)
        parity, place = lax.rem(group, 2), lax.div(group, 2)
        rows_at = pl.ds(pl.multiple_of(place * cap, cap), cap)
        for bits in range(owners):
            for i in range(local):
                at = bits * held + i * cap
                out_refs[bits][parity, i, rows_at, :] = sent[at : at + cap]

    message = arr((2, local, pair_rows, width))

    def dispatch_x_body(*refs):
        x_refs, cot_ref, score_ref = refs[:groups], refs[groups], refs[groups + 1]
        outs = refs[groups + 2 :]
        send_refs, d_refs = outs[:owners], outs[owners : owners + groups]
        slot_ref, mix_ref, weighted_ref = outs[owners + groups :]
        for step in range(groups):
            group = group_at(-step)
            slot = slots_row(x_refs[step][toks : toks + extra, 0:toks][0:1].astype(F32))
            slot_ref[pl.ds(group * 8, 8), :] = jnp.broadcast_to(slot, (8, toks))
            send_rows(picker(slot), x_refs[step][0:toks, :], group, send_refs)
        score = score_ref[...]
        mix = score[:, 0:1] / jnp.sum(score, axis=1, keepdims=True)
        mix_ref[...] = jnp.broadcast_to(mix, mix_ref.shape)
        weighted_ref[...] = (mix * cot_ref[...].astype(F32)).astype(BF16)
        for step in range(groups):
            d_refs[step][...] = weighted_ref[:, columns_at(step)]

    got = call(
        dispatch_x_body,
        [message] * owners
        + [arr((toks, width))] * groups
        + [arr((groups * 8, toks), jnp.int32), arr((toks, 128), F32)],
        [*x_got, cotangent, scores],
        scratch=[pltpu.VMEM((toks, model_width), BF16)],
        flops=2 * groups * slot_total * toks * width,
    )
    x_send, d_pack = got[:owners], got[owners : owners + groups]
    slots, mix_wide = got[owners + groups :]
    rows_x = [x_send[0]] + [swap(x_send[bits], bits) for bits in range(1, owners)]
    d_got = [d_pack[0]] + [shift(d_pack[step], step) for step in range(1, groups)]

    def half_specs(half):
        return [pl.BlockSpec((1, local, pair_rows, width), lambda *_: (half, 0, 0, 0))] * owners

    full = pl.BlockSpec(memory_space=pltpu.VMEM)

    def expert_rows(refs, i):
        return jnp.concatenate([r[0, i] for r in refs], axis=0)

    piece = arr((half_rows, units))
    piece_flops = 2 * half_rows * units * width

    def part_into(out_ref, row_refs, w_ref, product):
        for i in range(local):
            out_ref[i * block : (i + 1) * block, :] = product(
                expert_rows(row_refs, i), w_ref[i]
            ).astype(BF16)

    def first_body(*refs):
        rows, gate_ref, up_ref = refs[:owners], refs[owners], refs[owners + 1]
        part_into(refs[-2], rows, gate_ref, mm)
        part_into(refs[-1], rows, up_ref, mm)

    part = {}
    part["g0"], part["u0"] = call(
        first_body,
        [piece, piece],
        [*rows_x, w_gate, w_up],
        specs=half_specs(0) + [full, full],
        flops=2 * piece_flops,
    )

    order = ["g0", "u0", "g1", "u1", "b0", "b1"]
    near, far, back, pair, total = {}, {}, {}, {}, {}
    near["g0"], near["u0"] = near_hop(part["g0"]), near_hop(part["u0"])

    def slot_call(number, rows=None, half=0, weight=None, product=None):
        take = order[number] if number < len(order) else None
        last = order[number - 1] if number > 0 else None
        ins, outs = [], []
        if take:
            ins += [part[take], near[take]]
            outs.append(piece)
        if last:
            ins += [pair[last], far[last]]
            outs.append(piece)
        specs = [full] * len(ins)
        if rows is not None:
            ins += [*rows, weight]
            specs += half_specs(half) + [full]
            outs.append(piece)
        count = len(ins)

        def body(*refs):
            at, to = 0, count
            for _ in range(bool(take) + bool(last)):
                refs[to][...] = (refs[at][...].astype(F32) + refs[at + 1][...].astype(F32)).astype(
                    BF16
                )
                at, to = at + 2, to + 1
            if rows is not None:
                part_into(refs[to], refs[at : at + owners], refs[at + owners], product)

        got = list(
            call(body, outs, ins, specs=specs, flops=piece_flops if rows is not None else 0)
        )
        if take:
            pair[take] = got.pop(0)
            far[take] = far_hop(pair[take])
        if last:
            total[last] = got.pop(0)
            back[last] = back_hop(total[last])
        if rows is not None:
            name = order[number + 2]
            part[name] = got.pop(0)
            near[name] = near_hop(part[name])

    slot_call(0, rows_x, 1, w_gate, mm)

    def dispatch_d_body(*refs):
        d_refs, slot_ref, out_refs = refs[:groups], refs[groups], refs[groups + 1 :]
        for step in range(groups):
            group = group_at(-step)
            slot = slot_ref[pl.ds(group * 8, 8), :][0:1]
            send_rows(picker(slot), d_refs[step][...], group, out_refs)

    d_send = call(
        dispatch_d_body,
        [message] * owners,
        [*d_got, slots],
        flops=2 * groups * slot_total * toks * width,
    )
    rows_d = [d_send[0]] + [swap(d_send[bits], bits) for bits in range(1, owners)]

    slot_call(1, rows_x, 1, w_up, mm)
    slot_call(2, rows_d, 0, w_down, mm_nt)
    slot_call(3, rows_d, 1, w_down, mm_nt)
    slot_call(4)
    slot_call(5)

    def summed(total_ref, back_ref):
        place = lax.axis_index("dp")
        at_end = (place == 0) | (place == groups - 1)
        return jnp.where(at_end, back_ref[...], total_ref[...]).astype(F32)

    def both(name):
        return [total[name], back[name]]

    def spread(refs, half, i, value):
        for bits in range(owners):
            rows = value[bits * pair_rows : (bits + 1) * pair_rows]
            if half is None:
                refs[bits][i] = rows
            else:
                refs[bits][half, i] = rows

    def out_body(*refs):
        w_ref, outs = refs[8], refs[9:]
        hidden_refs, out_refs = outs[:2], outs[2:]
        for half in range(2):
            t = refs[4 * half : 4 * half + 4]
            gate, up = summed(t[0], t[1]), summed(t[2], t[3])
            hidden_refs[half][...] = (gate * jax.nn.sigmoid(gate) * up).astype(BF16)
            for i in range(local):
                rows = hidden_refs[half][i * block : (i + 1) * block, :]
                spread(out_refs, half, i, mm(rows, w_ref[i]).astype(BF16))

    got = call(
        out_body,
        [piece, piece] + [message] * owners,
        [*both("g0"), *both("u0"), *both("g1"), *both("u1"), w_down],
        flops=2 * piece_flops,
    )
    hidden, out_send = got[:2], got[2:]
    out_got = [out_send[0]] + [swap(out_send[bits], bits) for bits in range(1, owners)]

    slot_call(6)

    half_message = arr((local, pair_rows, width))

    def combine(slot_ref, block_of, out_refs, sum_ref):
        for group in range(groups):
            place = group // 2 * cap
            rows = [
                block_of(bits, group % 2, i, slice(place, place + cap))
                for bits in range(owners)
                for i in range(local)
            ]
            pick = picker(slot_ref[group * 8 : group * 8 + 1, :])
            sum_ref[group] = mm_tn(pick, jnp.concatenate(rows, axis=0)).astype(BF16)
        for step in range(groups):
            out_refs[step][...] = sum_ref[group_at(-step)]

    def in_call(half, with_out):
        names = [f"g{half}", f"u{half}", f"b{half}"]
        ins = [a for n in names for a in both(n)] + [w_gate, w_up]
        outs = [piece, piece] + [half_message] * owners
        scratch = []
        if with_out:
            ins += [*out_got, slots]
            outs += [arr((toks, width))] * groups
            scratch = [pltpu.VMEM((groups, toks, width), BF16)]
        count = len(ins)

        def body(*refs):
            gate, up, grad = (summed(refs[2 * n], refs[2 * n + 1]) for n in range(3))
            gate_w, up_w = refs[6], refs[7]
            act_refs, in_refs = refs[count : count + 2], refs[count + 2 : count + 2 + owners]
            sigma = jax.nn.sigmoid(gate)
            act_refs[0][...] = (grad * up * sigma * (1.0 + gate * (1.0 - sigma))).astype(BF16)
            act_refs[1][...] = (grad * (gate * sigma)).astype(BF16)
            for i in range(local):
                rows = slice(i * block, (i + 1) * block)
                into = mm_nt(act_refs[0][rows, :], gate_w[i]) + mm_nt(
                    act_refs[1][rows, :], up_w[i]
                )
                spread(in_refs, None, i, into.astype(BF16))
            if with_out:
                got_refs, slot_ref = refs[8 : 8 + owners], refs[8 + owners]
                combine(
                    slot_ref,
                    lambda bits, parity, i, rows: got_refs[bits][parity, i, rows, :],
                    refs[count + 2 + owners : count + 2 + owners + groups],
                    refs[-1],
                )

        return call(body, outs, ins, scratch=scratch, flops=2 * piece_flops)

    got0 = in_call(0, False)
    in_got0 = [got0[2]] + [swap(got0[2 + bits], bits) for bits in range(1, owners)]
    got1 = in_call(1, True)
    in_got1 = [got1[2]] + [swap(got1[2 + bits], bits) for bits in range(1, owners)]
    out_tok = got1[2 + owners :]
    out_chunk = [out_tok[0]] + [shift(out_tok[step], -step) for step in range(1, groups)]

    def in_tokens_body(*refs):
        halves = (refs[:owners], refs[owners : 2 * owners])
        combine(
            refs[2 * owners],
            lambda bits, parity, i, rows: halves[parity][bits][i, rows, :],
            refs[2 * owners + 1 : 2 * owners + 1 + groups],
            refs[-1],
        )

    in_tok = call(
        in_tokens_body,
        [arr((toks, width))] * groups,
        [*in_got0, *in_got1, slots],
        scratch=[pltpu.VMEM((groups, toks, width), BF16)],
        flops=2 * groups * slot_total * toks * width,
    )
    in_chunk = [in_tok[0]] + [shift(in_tok[step], -step) for step in range(1, groups)]

    per_part = groups // 2
    part_width = per_part * width

    def assemble_body(*refs):
        chunk_refs, give_ref, keep_ref, whole_ref = refs[:groups], *refs[groups:]
        for step in range(groups):
            whole_ref[group_at(step)] = chunk_refs[step][...]
        mine = lax.axis_index("tensor")
        for j in range(per_part):
            at = slice(j * width, (j + 1) * width)
            give_ref[:, at] = whole_ref[(1 - mine) * per_part + j]
            keep_ref[:, at] = whole_ref[mine * per_part + j]

    def assemble(chunks):
        give, keep = call(
            assemble_body,
            [arr((toks, part_width))] * 2,
            chunks,
            scratch=[pltpu.VMEM((groups, toks, width), BF16)],
        )
        other = lax.ppermute(give, "tensor", [(0, 1), (1, 0)])
        return keep.astype(F32) + other.astype(F32)

    output = (mix_wide[:, 0:1] * assemble(out_chunk)).astype(BF16)
    grad_tokens = assemble(in_chunk).astype(BF16)

    def weight_grad(left_body, ins, shape):
        def body(*refs):
            for i in range(local):
                left, right = left_body(refs, i)
                refs[-1][i] = mm_tn(left, right)

        return call(body, [arr(shape, F32)], ins, flops=2 * piece_flops)[0]

    def all_rows(refs, i):
        return jnp.concatenate([r[half, i] for half in range(2) for r in refs], axis=0)

    def all_units(refs, i):
        return jnp.concatenate([r[i * block : (i + 1) * block, :] for r in refs], axis=0)

    def by_rows(refs, i):
        return all_rows(refs[:owners], i), all_units(refs[owners : owners + 2], i)

    def by_units(refs, i):
        right, left = by_rows(refs, i)
        return left, right

    grad_gate = weight_grad(by_rows, [*rows_x, got0[0], got1[0]], w_gate.shape)
    grad_up = weight_grad(by_rows, [*rows_x, got0[1], got1[1]], w_up.shape)
    grad_down = weight_grad(by_units, [*rows_d, *hidden], w_down.shape)
    return (output, grad_tokens, grad_gate, grad_up, grad_down)


def on_device(tokens, cotangent, scores, routes, w_gate, w_up, w_down):
    owners = lax.axis_size("expert")
    toks = tokens.shape[0]
    cap = min(toks, 2 * toks // (w_gate.shape[0] * owners))
    held = w_gate.shape[0] * cap
    fits = (
        lax.axis_size("dp") == 4
        and lax.axis_size("tensor") == 2
        and owners == 4
        and cap % 16 == 0
        and held & (held - 1) == 0
        and toks == 128
        and w_gate.shape[1] % 128 == 0
        and w_gate.shape[2] % 128 == 0
    )
    form = kernel_form if fits else plain_form
    return form(tokens, cotangent, scores, routes, w_gate, w_up, w_down)


def solution(mesh):
    in_specs = (
        P(("dp", "expert"), None),
        P(("dp", "expert"), None),
        P(("dp", "expert"), None),
        P(("dp", "expert"), None),
        P("expert", "dp", "tensor"),
        P("expert", "dp", "tensor"),
        P("expert", "tensor", "dp"),
    )
    out_specs = (
        P(("dp", "expert"), "tensor"),
        P(("dp", "expert"), "tensor"),
        P("expert", "dp", "tensor"),
        P("expert", "dp", "tensor"),
        P("expert", "tensor", "dp"),
    )
    return jax.shard_map(
        on_device, mesh=mesh, in_specs=in_specs, out_specs=out_specs, check_vma=False
    )
```

```python
import jax
import jax.numpy as jnp
from jax import lax
from jax.experimental import pallas as pl
from jax.experimental.pallas import tpu as pltpu
from jax.sharding import PartitionSpec as P

F32 = jnp.float32
BF16 = jnp.bfloat16


def dot(eq, a, b):
    return jnp.einsum(eq, a, b, preferred_element_type=F32)


def plain_form(tokens, cotangent, scores, routes, w_gate, w_up, w_down):
    tok_count, model_width = tokens.shape
    owners = lax.axis_size("expert")
    groups = lax.axis_size("dp")
    sharers = lax.axis_size("tensor")
    local_count = w_gate.shape[0]
    expert_count = local_count * owners
    capacity = min(tok_count, 2 * tok_count // expert_count)
    held = local_count * capacity
    width = model_width // groups
    my_group = lax.axis_index("dp")
    my_owner = lax.axis_index("expert")
    my_part = lax.axis_index("tensor")

    def shift(value, step):
        if step % groups == 0:
            return value
        return lax.ppermute(value, "dp", [(j, (j + step) % groups) for j in range(groups)])

    def swap(value, bits):
        if bits == 0:
            return value
        return lax.ppermute(value, "expert", [(j, j ^ bits) for j in range(owners)])

    def chunks_out(rows):
        parts = []
        for step in range(groups):
            start = lax.rem(my_group + step, groups) * width
            parts.append(shift(lax.dynamic_slice(rows, (0, start), (tok_count, width)), step))
        return parts

    def picked(stack, index):
        return lax.dynamic_index_in_dim(stack, lax.rem(index + groups, groups), 0, keepdims=False)

    def by_group(parts):
        stack = jnp.stack(parts)
        return jnp.stack([picked(stack, my_group - g) for g in range(groups)])

    routes_all = by_group([shift(routes[:, 0], step) for step in range(groups)])
    x_chunk = by_group(chunks_out(tokens))
    mix = scores[:, :1] / jnp.sum(scores, axis=1, keepdims=True)
    weighted = (mix * cotangent.astype(F32)).astype(BF16)
    d_chunk = by_group(chunks_out(weighted))

    member = (routes_all[:, :, None] == jnp.arange(expert_count, dtype=jnp.int32)).astype(F32)
    earlier = jnp.tril(jnp.ones((tok_count, tok_count), BF16), -1)
    before = dot("ab,gbe->gae", earlier, member.astype(BF16))
    place = jnp.sum(before * member, axis=2).astype(jnp.int32)
    slot_ids = routes_all * capacity + place

    def picker(bits):
        base = (my_owner ^ bits) * held
        wanted = base + jnp.arange(held, dtype=jnp.int32).reshape(local_count, 1, capacity, 1)
        return (slot_ids[None, :, None, :] == wanted).astype(BF16)

    pickers = [picker(bits) for bits in range(owners)]

    def dispatch(chunk):
        got = []
        for bits in range(owners):
            send = dot("igct,gtk->igck", pickers[bits], chunk).astype(BF16)
            got.append(swap(send.reshape(local_count, groups * capacity, width), bits))
        return [jnp.concatenate([g[i] for g in got], axis=0) for i in range(local_count)]

    rows_x = dispatch(x_chunk)
    rows_d = dispatch(d_chunk)

    def line_sum(part):
        part = part.astype(BF16)
        if groups != 4:
            return lax.psum(part, "dp").astype(F32)
        near = lax.ppermute(part, "dp", [(0, 1), (3, 2)])
        pair = part.astype(F32) + near.astype(F32)
        far = lax.ppermute(pair.astype(BF16), "dp", [(1, 2), (2, 1)])
        total = (pair + far.astype(F32)).astype(BF16)
        back = lax.ppermute(total, "dp", [(1, 0), (2, 3)])
        at_end = (my_group == 0) | (my_group == groups - 1)
        return jnp.where(at_end, back, total).astype(F32)

    experts = range(local_count)
    gate_act, up_act, back_grad = {}, {}, {}
    for i in experts:
        gate_act[i] = line_sum(dot("rk,kf->rf", rows_x[i], w_gate[i]))
        up_act[i] = line_sum(dot("rk,kf->rf", rows_x[i], w_up[i]))
    for i in experts:
        back_grad[i] = line_sum(dot("rk,fk->rf", rows_d[i], w_down[i]))

    part_out, part_in, grad_gate, grad_up, grad_down = [], [], [], [], []
    for i in experts:
        sigma = jax.nn.sigmoid(gate_act[i])
        silu_act = gate_act[i] * sigma
        hidden = (silu_act * up_act[i]).astype(BF16)
        act_gate = (
            back_grad[i] * up_act[i] * sigma * (1.0 + gate_act[i] * (1.0 - sigma))
        ).astype(BF16)
        act_up = (back_grad[i] * silu_act).astype(BF16)
        part_out.append(dot("rf,fk->rk", hidden, w_down[i]).astype(BF16))
        into = dot("rf,kf->rk", act_gate, w_gate[i]) + dot("rf,kf->rk", act_up, w_up[i])
        part_in.append(into.astype(BF16))
        grad_gate.append(dot("rk,rf->kf", rows_x[i], act_gate))
        grad_up.append(dot("rk,rf->kf", rows_x[i], act_up))
        grad_down.append(dot("rf,rk->fk", hidden, rows_d[i]))

    pick_all = jnp.stack(pickers)

    def combine(parts):
        rows = jnp.stack(parts).reshape(local_count, owners, groups, capacity, width)
        back = jnp.stack([swap(rows[:, bits], bits) for bits in range(owners)])
        sums = dot("bigct,bigck->gtk", pick_all, back).astype(BF16)
        mine = jnp.stack(
            [shift(picked(sums, my_group - step), -step) for step in range(groups)]
        )
        whole = jnp.concatenate([picked(mine, c - my_group) for c in range(groups)], axis=1)
        if sharers != 2:
            return lax.psum_scatter(whole, "tensor", scatter_dimension=1, tiled=True).astype(F32)
        half = model_width // 2
        give = lax.dynamic_slice(whole, (0, (1 - my_part) * half), (tok_count, half))
        keep = lax.dynamic_slice(whole, (0, my_part * half), (tok_count, half))
        return keep.astype(F32) + lax.ppermute(give, "tensor", [(0, 1), (1, 0)]).astype(F32)

    output = (mix * combine(part_out)).astype(BF16)
    grad_tokens = combine(part_in).astype(BF16)
    return (output, grad_tokens, jnp.stack(grad_gate), jnp.stack(grad_up), jnp.stack(grad_down))


VMEM_LIMIT = 48 * 1024 * 1024


def call(body, outs, ins, scratch=(), flops=0, specs=None):
    moved = sum(a.size * a.dtype.itemsize for a in ins)
    moved += sum(o.size * o.dtype.itemsize for o in outs)
    many = pl.BlockSpec(memory_space=pltpu.VMEM)
    return pl.pallas_call(
        body,
        out_shape=outs,
        grid=() if specs is None else (1,),
        in_specs=[many] * len(ins) if specs is None else specs,
        out_specs=[many] * len(outs),
        scratch_shapes=list(scratch),
        compiler_params=pltpu.CompilerParams(vmem_limit_bytes=VMEM_LIMIT),
        cost_estimate=pl.CostEstimate(flops=flops, bytes_accessed=moved, transcendentals=0),
    )(*ins)


def arr(shape, dtype=BF16):
    return jax.ShapeDtypeStruct(shape, dtype)


def mm(a, b):
    return jnp.dot(a, b, preferred_element_type=F32)


def mm_nt(a, b):
    return lax.dot_general(a, b, (((1,), (1,)), ((), ())), preferred_element_type=F32)


def mm_tn(a, b):
    return lax.dot_general(a, b, (((0,), (0,)), ((), ())), preferred_element_type=F32)


def kernel_form(tokens, cotangent, scores, routes, w_gate, w_up, w_down):
    toks, model_width = tokens.shape
    owners, groups = lax.axis_size("expert"), lax.axis_size("dp")
    local, width, units = w_gate.shape
    expert_count = local * owners
    cap = min(toks, 2 * toks // expert_count)
    held = local * cap
    slot_total = expert_count * cap
    pair_rows = groups // 2 * cap
    half_rows = local * owners * pair_rows
    block = owners * pair_rows
    extra = 16

    def shift(value, step):
        return lax.ppermute(value, "dp", [(j, (j + step) % groups) for j in range(groups)])

    def swap(value, bits):
        return lax.ppermute(value, "expert", [(j, j ^ bits) for j in range(owners)])

    def near_hop(value):
        return lax.ppermute(value, "dp", [(0, 1), (3, 2)])

    def far_hop(value):
        return lax.ppermute(value, "dp", [(1, 2), (2, 1)])

    def back_hop(value):
        return lax.ppermute(value, "dp", [(1, 0), (2, 3)])

    def group_at(step):
        return lax.rem(lax.axis_index("dp") + step + groups, groups)

    def columns_at(step):
        return pl.ds(pl.multiple_of(group_at(step) * width, width), width)

    def pack_body(tok_ref, route_ref, *out_refs):
        row = lax.broadcasted_iota(jnp.int32, (extra, toks), 0)
        line = jnp.broadcast_to(route_ref[...].astype(F32), (extra, toks))
        line = jnp.where(row == 0, line, 0.0).astype(BF16)
        for step in range(groups):
            out = out_refs[step]
            out[0:toks, :] = tok_ref[:, columns_at(step)]
            out[toks : toks + extra, :] = jnp.zeros((extra, width), BF16)
            out[toks : toks + extra, 0:toks] = line

    x_pack = call(
        pack_body, [arr((toks + extra, width))] * groups, [tokens, routes.reshape(1, toks)]
    )
    x_got = [x_pack[0]] + [shift(x_pack[step], step) for step in range(1, groups)]

    def slots_row(line):
        first = lax.broadcasted_iota(jnp.int32, (toks, toks), 0)
        second = lax.broadcasted_iota(jnp.int32, (toks, toks), 1)
        whole = jnp.broadcast_to(line, (toks, toks))
        column = jnp.sum(jnp.where(first == second, whole, 0.0), axis=1, keepdims=True)
        same = (column == whole) & (first < second)
        place = jnp.sum(jnp.where(same, 1.0, 0.0), axis=0, keepdims=True)
        slot = (line * float(cap) + place).astype(jnp.int32)
        return slot ^ (lax.axis_index("expert") * held)

    def picker(slot):
        row = lax.broadcasted_iota(jnp.int32, (slot_total, toks), 0)
        return jnp.where(row == jnp.broadcast_to(slot, (slot_total, toks)), 1.0, 0.0).astype(BF16)

    def send_rows(pick, rows, group, out_refs):
        sent = mm(pick, rows).astype(BF16)
        parity, place = lax.rem(group, 2), lax.div(group, 2)
        rows_at = pl.ds(pl.multiple_of(place * cap, cap), cap)
        for bits in range(owners):
            for i in range(local):
                at = bits * held + i * cap
                out_refs[bits][parity, i, rows_at, :] = sent[at : at + cap]

    message = arr((2, local, pair_rows, width))

    def dispatch_x_body(*refs):
        x_refs, cot_ref, score_ref = refs[:groups], refs[groups], refs[groups + 1]
        outs = refs[groups + 2 :]
        send_refs, d_refs = outs[:owners], outs[owners : owners + groups]
        slot_ref, mix_ref, weighted_ref = outs[owners + groups :]
        for step in range(groups):
            group = group_at(-step)
            slot = slots_row(x_refs[step][toks : toks + extra, 0:toks][0:1].astype(F32))
            slot_ref[pl.ds(group * 8, 8), :] = jnp.broadcast_to(slot, (8, toks))
            send_rows(picker(slot), x_refs[step][0:toks, :], group, send_refs)
        score = score_ref[...]
        mix = score[:, 0:1] / jnp.sum(score, axis=1, keepdims=True)
        mix_ref[...] = jnp.broadcast_to(mix, mix_ref.shape)
        weighted_ref[...] = (mix * cot_ref[...].astype(F32)).astype(BF16)
        for step in range(groups):
            d_refs[step][...] = weighted_ref[:, columns_at(step)]

    got = call(
        dispatch_x_body,
        [message] * owners
        + [arr((toks, width))] * groups
        + [arr((groups * 8, toks), jnp.int32), arr((toks, 128), F32)],
        [*x_got, cotangent, scores],
        scratch=[pltpu.VMEM((toks, model_width), BF16)],
        flops=2 * groups * slot_total * toks * width,
    )
    x_send, d_pack = got[:owners], got[owners : owners + groups]
    slots, mix_wide = got[owners + groups :]
    rows_x = [x_send[0]] + [swap(x_send[bits], bits) for bits in range(1, owners)]
    d_got = [d_pack[0]] + [shift(d_pack[step], step) for step in range(1, groups)]

    full = pl.BlockSpec(memory_space=pltpu.VMEM)
    piece = arr((half_rows, units))
    piece_flops = 2 * half_rows * units * width
    dispatch_flops = 2 * groups * slot_total * toks * width
    packed = arr((2, local, block, width))
    half_packed = pl.BlockSpec((1, local, block, width), lambda *_: (0, 0, 0, 0))
    other_packed = pl.BlockSpec((1, local, block, width), lambda *_: (1, 0, 0, 0))

    def pack_rows(out_ref, refs):
        for half in range(2):
            for i in range(local):
                for bits in range(owners):
                    at = slice(bits * pair_rows, (bits + 1) * pair_rows)
                    out_ref[half, i, at, :] = refs[bits][half, i]

    def part_into(out_ref, rows_ref, w_ref, product, half=0):
        for i in range(local):
            out_ref[i * block : (i + 1) * block, :] = product(rows_ref[half, i], w_ref[i]).astype(
                BF16
            )

    def first_body(*refs):
        x_refs, gate_ref, up_ref = refs[:owners], refs[owners], refs[owners + 1]
        d_refs, slot_ref = refs[owners + 2 : owners + 2 + groups], refs[owners + 2 + groups]
        outs = refs[owners + 3 + groups :]
        pack_rows(outs[2], x_refs)
        part_into(outs[0], outs[2], gate_ref, mm)
        part_into(outs[1], outs[2], up_ref, mm)
        for step in range(groups):
            group = group_at(-step)
            slot = slot_ref[pl.ds(group * 8, 8), :][0:1]
            send_rows(picker(slot), d_refs[step][...], group, outs[3:])

    part = {}
    got = call(
        first_body,
        [piece, piece, packed] + [message] * owners,
        [*rows_x, w_gate, w_up, *d_got, slots],
        flops=2 * piece_flops + dispatch_flops,
    )
    part["g0"], part["u0"], packed_x = got[:3]
    d_send = got[3:]

    order = ["g0", "u0", "g1", "u1", "b0", "b1"]
    near, far, back, pair, total, final = {}, {}, {}, {}, {}, {}
    near["g0"], near["u0"] = near_hop(part["g0"]), near_hop(part["u0"])
    rows_d = [d_send[0]] + [swap(d_send[bits], bits) for bits in range(1, owners)]

    def at_end():
        place = lax.axis_index("dp")
        return (place == 0) | (place == groups - 1)

    def slot_call(number, rows=None, half=0, weight=None, product=None, unpacked=None):
        take = order[number] if number < len(order) else None
        last = order[number - 1] if 0 < number <= len(order) else None
        done = order[number - 2] if 1 < number else None
        ins, outs = [], []
        for name, left, right in ((take, part, near), (last, pair, far), (done, total, back)):
            if name:
                ins += [left[name], right[name]]
                outs.append(piece)
        specs = [full] * len(ins)
        if rows is not None:
            ins += [rows, weight]
            specs += [other_packed if half else half_packed, full]
            outs.append(piece)
        if unpacked is not None:
            ins += unpacked
            specs += [full] * owners
            outs.append(packed)
        count = len(ins)

        def body(*refs):
            at, to = 0, count
            for name in (take, last):
                if name:
                    both = refs[at][...].astype(F32) + refs[at + 1][...].astype(F32)
                    refs[to][...] = both.astype(BF16)
                    at, to = at + 2, to + 1
            if done:
                refs[to][...] = jnp.where(at_end(), refs[at + 1][...], refs[at][...])
                at, to = at + 2, to + 1
            if rows is not None:
                part_into(refs[to], refs[at], refs[at + 1], product)
                at, to = at + 2, to + 1
            if unpacked is not None:
                pack_rows(refs[to], refs[at : at + owners])

        got = list(
            call(body, outs, ins, specs=specs, flops=piece_flops if rows is not None else 0)
        )
        if take:
            pair[take] = got.pop(0)
            far[take] = far_hop(pair[take])
        if last:
            total[last] = got.pop(0)
            back[last] = back_hop(total[last])
        if done:
            final[done] = got.pop(0)
        if rows is not None:
            name = order[number + 2]
            part[name] = got.pop(0)
            near[name] = near_hop(part[name])
        return got

    (packed_d,) = slot_call(0, packed_x, 1, w_gate, mm, unpacked=rows_d)
    slot_call(1, packed_x, 1, w_up, mm)
    slot_call(2, packed_d, 0, w_down, mm_nt)
    slot_call(3, packed_d, 1, w_down, mm_nt)
    slot_call(4)
    slot_call(5)

    def spread(refs, half, i, value):
        for bits in range(owners):
            rows = value[bits * pair_rows : (bits + 1) * pair_rows]
            if half is None:
                refs[bits][i] = rows
            else:
                refs[bits][half, i] = rows

    def out_body(*refs):
        w_ref, outs = refs[4], refs[5:]
        hidden_refs, out_refs = outs[:2], outs[2:]
        for half in range(2):
            gate, up = (refs[2 * half + n][...].astype(F32) for n in range(2))
            hidden_refs[half][...] = (gate * jax.nn.sigmoid(gate) * up).astype(BF16)
            for i in range(local):
                rows = hidden_refs[half][i * block : (i + 1) * block, :]
                spread(out_refs, half, i, mm(rows, w_ref[i]).astype(BF16))

    got = call(
        out_body,
        [piece, piece] + [message] * owners,
        [final["g0"], final["u0"], final["g1"], final["u1"], w_down],
        flops=2 * piece_flops,
    )
    hidden, out_send = got[:2], got[2:]
    out_got = [out_send[0]] + [swap(out_send[bits], bits) for bits in range(1, owners)]

    slot_call(6)

    half_message = arr((local, pair_rows, width))

    def combined(slot_ref, group, block_of):
        place = group // 2 * cap
        rows = [
            block_of(bits, i, slice(place, place + cap))
            for bits in range(owners)
            for i in range(local)
        ]
        pick = picker(slot_ref[group * 8 : group * 8 + 1, :])
        return mm_tn(pick, jnp.concatenate(rows, axis=0)).astype(BF16)

    def in_call(half):
        ins = [final[f"g{half}"], final[f"u{half}"]]
        ins += [final["b0"]] if half == 0 else [total["b1"], back["b1"]]
        ins += [w_gate, w_up]
        count = len(ins)

        def body(*refs):
            gate, up = refs[0][...].astype(F32), refs[1][...].astype(F32)
            grad = refs[2][...]
            if half == 1:
                grad = jnp.where(at_end(), refs[3][...], grad)
            grad = grad.astype(F32)
            gate_w, up_w = refs[count - 2], refs[count - 1]
            act_refs, in_refs = refs[count : count + 2], refs[count + 2 :]
            sigma = jax.nn.sigmoid(gate)
            act_refs[0][...] = (grad * up * sigma * (1.0 + gate * (1.0 - sigma))).astype(BF16)
            act_refs[1][...] = (grad * (gate * sigma)).astype(BF16)
            for i in range(local):
                rows = slice(i * block, (i + 1) * block)
                into = mm_nt(act_refs[0][rows, :], gate_w[i]) + mm_nt(
                    act_refs[1][rows, :], up_w[i]
                )
                spread(in_refs, None, i, into.astype(BF16))

        got = call(
            body, [piece, piece] + [half_message] * owners, ins, flops=2 * piece_flops
        )
        sent = got[2:]
        return got[:2], [sent[0]] + [swap(sent[bits], bits) for bits in range(1, owners)]

    acts0, in_got0 = in_call(0)
    acts1, in_got1 = in_call(1)

    def tokens_body(*refs):
        o_refs, i_refs, slot_ref = refs[:owners], refs[owners : 2 * owners], refs[2 * owners]
        outs = refs[2 * owners + 2 :]
        sum_ref = refs[-1]
        for group in range(groups):
            sum_ref[group] = combined(
                slot_ref, group, lambda bits, i, rows: o_refs[bits][group % 2, i, rows, :]
            )
        for group in range(0, groups, 2):
            outs[groups][group // 2] = combined(
                slot_ref, group, lambda bits, i, rows: i_refs[bits][i, rows, :]
            )
        for step in range(groups):
            outs[step][...] = sum_ref[group_at(-step)]

    got = call(
        tokens_body,
        [arr((toks, width))] * groups + [arr((groups // 2, toks, width))],
        [*out_got, *in_got0, slots, acts1[0]],
        scratch=[pltpu.VMEM((groups, toks, width), BF16)],
        flops=2 * dispatch_flops,
    )
    out_tok, in_even = got[:groups], got[groups]
    out_chunk = [out_tok[0]] + [shift(out_tok[step], -step) for step in range(1, groups)]

    def in_tokens_body(*refs):
        i_refs, even_ref, slot_ref = refs[:owners], refs[owners], refs[owners + 1]
        sum_ref = refs[-1]
        for group in range(groups):
            if group % 2 == 0:
                sum_ref[group] = even_ref[group // 2]
            else:
                sum_ref[group] = combined(
                    slot_ref, group, lambda bits, i, rows: i_refs[bits][i, rows, :]
                )
        for step in range(groups):
            refs[owners + 2 + step][...] = sum_ref[group_at(-step)]

    in_tok = call(
        in_tokens_body,
        [arr((toks, width))] * groups,
        [*in_got1, in_even, slots],
        scratch=[pltpu.VMEM((groups, toks, width), BF16)],
        flops=dispatch_flops,
    )
    in_chunk = [in_tok[0]] + [shift(in_tok[step], -step) for step in range(1, groups)]

    per_part = groups // 2
    part_width = per_part * width

    def assemble_body(*refs):
        chunk_refs, give_ref, keep_ref, whole_ref = refs[:groups], *refs[groups:]
        for step in range(groups):
            whole_ref[group_at(step)] = chunk_refs[step][...]
        mine = lax.axis_index("tensor")
        for j in range(per_part):
            at = slice(j * width, (j + 1) * width)
            give_ref[:, at] = whole_ref[(1 - mine) * per_part + j]
            keep_ref[:, at] = whole_ref[mine * per_part + j]

    def assemble(chunks):
        give, keep = call(
            assemble_body,
            [arr((toks, part_width))] * 2,
            chunks,
            scratch=[pltpu.VMEM((groups, toks, width), BF16)],
        )
        other = lax.ppermute(give, "tensor", [(0, 1), (1, 0)])
        return keep.astype(F32) + other.astype(F32)

    output = (mix_wide[:, 0:1] * assemble(out_chunk)).astype(BF16)
    grad_tokens = assemble(in_chunk).astype(BF16)

    def weight_grad(rows, acts, shape, rows_first):
        def body(*refs):
            for i in range(local):
                part_sum = None
                for half in range(2):
                    left, right = refs[0][half, i], refs[1 + half][i * block : (i + 1) * block, :]
                    if not rows_first:
                        left, right = right, left
                    term = mm_tn(left, right)
                    part_sum = term if part_sum is None else part_sum + term
                refs[-1][i] = part_sum

        return call(body, [arr(shape, F32)], [rows, *acts], flops=2 * piece_flops)[0]

    grad_gate = weight_grad(packed_x, [acts0[0], acts1[0]], w_gate.shape, True)
    grad_up = weight_grad(packed_x, [acts0[1], acts1[1]], w_up.shape, True)
    grad_down = weight_grad(packed_d, hidden, w_down.shape, False)
    return (output, grad_tokens, grad_gate, grad_up, grad_down)


def on_device(tokens, cotangent, scores, routes, w_gate, w_up, w_down):
    owners = lax.axis_size("expert")
    toks = tokens.shape[0]
    cap = min(toks, 2 * toks // (w_gate.shape[0] * owners))
    held = w_gate.shape[0] * cap
    fits = (
        lax.axis_size("dp") == 4
        and lax.axis_size("tensor") == 2
        and owners == 4
        and cap % 16 == 0
        and held & (held - 1) == 0
        and toks == 128
        and w_gate.shape[1] % 128 == 0
        and w_gate.shape[2] % 128 == 0
    )
    form = kernel_form if fits else plain_form
    return form(tokens, cotangent, scores, routes, w_gate, w_up, w_down)


def solution(mesh):
    in_specs = (
        P(("dp", "expert"), None),
        P(("dp", "expert"), None),
        P(("dp", "expert"), None),
        P(("dp", "expert"), None),
        P("expert", "dp", "tensor"),
        P("expert", "dp", "tensor"),
        P("expert", "tensor", "dp"),
    )
    out_specs = (
        P(("dp", "expert"), "tensor"),
        P(("dp", "expert"), "tensor"),
        P("expert", "dp", "tensor"),
        P("expert", "dp", "tensor"),
        P("expert", "tensor", "dp"),
    )
    return jax.shard_map(
        on_device, mesh=mesh, in_specs=in_specs, out_specs=out_specs, check_vma=False
    )
```

```python
import jax
import jax.numpy as jnp
from jax import lax
from jax.experimental import pallas as pl
from jax.experimental.pallas import tpu as pltpu
from jax.sharding import PartitionSpec as P

F32 = jnp.float32
BF16 = jnp.bfloat16


def dot(eq, a, b):
    return jnp.einsum(eq, a, b, preferred_element_type=F32)


def plain_form(tokens, cotangent, scores, routes, w_gate, w_up, w_down):
    tok_count, model_width = tokens.shape
    owners = lax.axis_size("expert")
    groups = lax.axis_size("dp")
    sharers = lax.axis_size("tensor")
    local_count = w_gate.shape[0]
    expert_count = local_count * owners
    capacity = min(tok_count, 2 * tok_count // expert_count)
    held = local_count * capacity
    width = model_width // groups
    my_group = lax.axis_index("dp")
    my_owner = lax.axis_index("expert")
    my_part = lax.axis_index("tensor")

    def shift(value, step):
        if step % groups == 0:
            return value
        return lax.ppermute(value, "dp", [(j, (j + step) % groups) for j in range(groups)])

    def swap(value, bits):
        if bits == 0:
            return value
        return lax.ppermute(value, "expert", [(j, j ^ bits) for j in range(owners)])

    def chunks_out(rows):
        parts = []
        for step in range(groups):
            start = lax.rem(my_group + step, groups) * width
            parts.append(shift(lax.dynamic_slice(rows, (0, start), (tok_count, width)), step))
        return parts

    def picked(stack, index):
        return lax.dynamic_index_in_dim(stack, lax.rem(index + groups, groups), 0, keepdims=False)

    def by_group(parts):
        stack = jnp.stack(parts)
        return jnp.stack([picked(stack, my_group - g) for g in range(groups)])

    routes_all = by_group([shift(routes[:, 0], step) for step in range(groups)])
    x_chunk = by_group(chunks_out(tokens))
    mix = scores[:, :1] / jnp.sum(scores, axis=1, keepdims=True)
    weighted = (mix * cotangent.astype(F32)).astype(BF16)
    d_chunk = by_group(chunks_out(weighted))

    member = (routes_all[:, :, None] == jnp.arange(expert_count, dtype=jnp.int32)).astype(F32)
    earlier = jnp.tril(jnp.ones((tok_count, tok_count), BF16), -1)
    before = dot("ab,gbe->gae", earlier, member.astype(BF16))
    place = jnp.sum(before * member, axis=2).astype(jnp.int32)
    slot_ids = routes_all * capacity + place

    def picker(bits):
        base = (my_owner ^ bits) * held
        wanted = base + jnp.arange(held, dtype=jnp.int32).reshape(local_count, 1, capacity, 1)
        return (slot_ids[None, :, None, :] == wanted).astype(BF16)

    pickers = [picker(bits) for bits in range(owners)]

    def dispatch(chunk):
        got = []
        for bits in range(owners):
            send = dot("igct,gtk->igck", pickers[bits], chunk).astype(BF16)
            got.append(swap(send.reshape(local_count, groups * capacity, width), bits))
        return [jnp.concatenate([g[i] for g in got], axis=0) for i in range(local_count)]

    rows_x = dispatch(x_chunk)
    rows_d = dispatch(d_chunk)

    def line_sum(part):
        part = part.astype(BF16)
        if groups != 4:
            return lax.psum(part, "dp").astype(F32)
        near = lax.ppermute(part, "dp", [(0, 1), (3, 2)])
        pair = part.astype(F32) + near.astype(F32)
        far = lax.ppermute(pair.astype(BF16), "dp", [(1, 2), (2, 1)])
        total = (pair + far.astype(F32)).astype(BF16)
        back = lax.ppermute(total, "dp", [(1, 0), (2, 3)])
        at_end = (my_group == 0) | (my_group == groups - 1)
        return jnp.where(at_end, back, total).astype(F32)

    experts = range(local_count)
    gate_act, up_act, back_grad = {}, {}, {}
    for i in experts:
        gate_act[i] = line_sum(dot("rk,kf->rf", rows_x[i], w_gate[i]))
        up_act[i] = line_sum(dot("rk,kf->rf", rows_x[i], w_up[i]))
    for i in experts:
        back_grad[i] = line_sum(dot("rk,fk->rf", rows_d[i], w_down[i]))

    part_out, part_in, grad_gate, grad_up, grad_down = [], [], [], [], []
    for i in experts:
        sigma = jax.nn.sigmoid(gate_act[i])
        silu_act = gate_act[i] * sigma
        hidden = (silu_act * up_act[i]).astype(BF16)
        act_gate = (
            back_grad[i] * up_act[i] * sigma * (1.0 + gate_act[i] * (1.0 - sigma))
        ).astype(BF16)
        act_up = (back_grad[i] * silu_act).astype(BF16)
        part_out.append(dot("rf,fk->rk", hidden, w_down[i]).astype(BF16))
        into = dot("rf,kf->rk", act_gate, w_gate[i]) + dot("rf,kf->rk", act_up, w_up[i])
        part_in.append(into.astype(BF16))
        grad_gate.append(dot("rk,rf->kf", rows_x[i], act_gate))
        grad_up.append(dot("rk,rf->kf", rows_x[i], act_up))
        grad_down.append(dot("rf,rk->fk", hidden, rows_d[i]))

    pick_all = jnp.stack(pickers)

    def combine(parts):
        rows = jnp.stack(parts).reshape(local_count, owners, groups, capacity, width)
        back = jnp.stack([swap(rows[:, bits], bits) for bits in range(owners)])
        sums = dot("bigct,bigck->gtk", pick_all, back).astype(BF16)
        mine = jnp.stack(
            [shift(picked(sums, my_group - step), -step) for step in range(groups)]
        )
        whole = jnp.concatenate([picked(mine, c - my_group) for c in range(groups)], axis=1)
        if sharers != 2:
            return lax.psum_scatter(whole, "tensor", scatter_dimension=1, tiled=True).astype(F32)
        half = model_width // 2
        give = lax.dynamic_slice(whole, (0, (1 - my_part) * half), (tok_count, half))
        keep = lax.dynamic_slice(whole, (0, my_part * half), (tok_count, half))
        return keep.astype(F32) + lax.ppermute(give, "tensor", [(0, 1), (1, 0)]).astype(F32)

    output = (mix * combine(part_out)).astype(BF16)
    grad_tokens = combine(part_in).astype(BF16)
    return (output, grad_tokens, jnp.stack(grad_gate), jnp.stack(grad_up), jnp.stack(grad_down))


VMEM_LIMIT = 48 * 1024 * 1024


def call(body, outs, ins, scratch=(), flops=0, specs=None):
    moved = sum(a.size * a.dtype.itemsize for a in ins)
    moved += sum(o.size * o.dtype.itemsize for o in outs)
    many = pl.BlockSpec(memory_space=pltpu.VMEM)
    return pl.pallas_call(
        body,
        out_shape=outs,
        grid=() if specs is None else (1,),
        in_specs=[many] * len(ins) if specs is None else specs,
        out_specs=[many] * len(outs),
        scratch_shapes=list(scratch),
        compiler_params=pltpu.CompilerParams(vmem_limit_bytes=VMEM_LIMIT),
        cost_estimate=pl.CostEstimate(flops=flops, bytes_accessed=moved, transcendentals=0),
    )(*ins)


def arr(shape, dtype=BF16):
    return jax.ShapeDtypeStruct(shape, dtype)


def mm(a, b):
    return jnp.dot(a, b, preferred_element_type=F32)


def mm_nt(a, b):
    return lax.dot_general(a, b, (((1,), (1,)), ((), ())), preferred_element_type=F32)


def mm_tn(a, b):
    return lax.dot_general(a, b, (((0,), (0,)), ((), ())), preferred_element_type=F32)


def kernel_form(tokens, cotangent, scores, routes, w_gate, w_up, w_down):
    toks, model_width = tokens.shape
    owners, groups = lax.axis_size("expert"), lax.axis_size("dp")
    local, width, units = w_gate.shape
    expert_count = local * owners
    cap = min(toks, 2 * toks // expert_count)
    held = local * cap
    slot_total = expert_count * cap
    pair_rows = groups // 2 * cap
    half_rows = local * owners * pair_rows
    block = owners * pair_rows
    extra = 16

    def shift(value, step):
        return lax.ppermute(value, "dp", [(j, (j + step) % groups) for j in range(groups)])

    def swap(value, bits):
        return lax.ppermute(value, "expert", [(j, j ^ bits) for j in range(owners)])

    inward, outward = [(0, 1), (3, 2)], [(1, 0), (2, 3)]

    def line_hop(value, pairs):
        return lax.ppermute(value, "dp", pairs)

    def group_at(step):
        return lax.rem(lax.axis_index("dp") + step + groups, groups)

    def columns_at(step):
        return pl.ds(pl.multiple_of(group_at(step) * width, width), width)

    def pack_body(tok_ref, route_ref, *out_refs):
        row = lax.broadcasted_iota(jnp.int32, (extra, toks), 0)
        line = jnp.broadcast_to(route_ref[...].astype(F32), (extra, toks))
        line = jnp.where(row == 0, line, 0.0).astype(BF16)
        for step in range(groups):
            out = out_refs[step]
            out[0:toks, :] = tok_ref[:, columns_at(step)]
            out[toks : toks + extra, :] = jnp.zeros((extra, width), BF16)
            out[toks : toks + extra, 0:toks] = line

    x_pack = call(
        pack_body, [arr((toks + extra, width))] * groups, [tokens, routes.reshape(1, toks)]
    )
    x_got = [x_pack[0]] + [shift(x_pack[step], step) for step in range(1, groups)]

    def slots_row(line):
        first = lax.broadcasted_iota(jnp.int32, (toks, toks), 0)
        second = lax.broadcasted_iota(jnp.int32, (toks, toks), 1)
        whole = jnp.broadcast_to(line, (toks, toks))
        column = jnp.sum(jnp.where(first == second, whole, 0.0), axis=1, keepdims=True)
        same = (column == whole) & (first < second)
        place = jnp.sum(jnp.where(same, 1.0, 0.0), axis=0, keepdims=True)
        slot = (line * float(cap) + place).astype(jnp.int32)
        return slot ^ (lax.axis_index("expert") * held)

    def picker(slot):
        row = lax.broadcasted_iota(jnp.int32, (slot_total, toks), 0)
        return jnp.where(row == jnp.broadcast_to(slot, (slot_total, toks)), 1.0, 0.0).astype(BF16)

    def send_rows(pick, rows, group, out_refs):
        sent = mm(pick, rows).astype(BF16)
        parity, place = lax.rem(group, 2), lax.div(group, 2)
        rows_at = pl.ds(pl.multiple_of(place * cap, cap), cap)
        for bits in range(owners):
            for i in range(local):
                at = bits * held + i * cap
                out_refs[bits][parity, i, rows_at, :] = sent[at : at + cap]

    message = arr((2, local, pair_rows, width))

    def weigh_body(x_ref, cot_ref, score_ref, *outs):
        d_refs, (line_ref, mix_ref, weighted_ref) = outs[:groups], outs[groups:]
        line_ref[...] = x_ref[...]
        score = score_ref[...]
        mix = score[:, 0:1] / jnp.sum(score, axis=1, keepdims=True)
        mix_ref[...] = jnp.broadcast_to(mix, mix_ref.shape)
        weighted_ref[...] = (mix * cot_ref[...].astype(F32)).astype(BF16)
        for step in range(groups):
            d_refs[step][...] = weighted_ref[:, columns_at(step)]

    got = call(
        weigh_body,
        [arr((toks, width))] * groups + [arr((toks + extra, width)), arr((toks, 128), F32)],
        [x_got[1], cotangent, scores],
        scratch=[pltpu.VMEM((toks, model_width), BF16)],
    )
    d_pack, (x_first, mix_wide) = got[:groups], got[groups:]
    d_got = [d_pack[0]] + [shift(d_pack[step], step) for step in range(1, groups)]

    def dispatch_x_body(*refs):
        x_refs, send_refs, slot_ref = refs[:groups], refs[groups:-1], refs[-1]
        for step in range(groups):
            group = group_at(-step)
            slot = slots_row(x_refs[step][toks : toks + extra, 0:toks][0:1].astype(F32))
            slot_ref[pl.ds(group * 8, 8), :] = jnp.broadcast_to(slot, (8, toks))
            send_rows(picker(slot), x_refs[step][0:toks, :], group, send_refs)

    got = call(
        dispatch_x_body,
        [message] * owners + [arr((groups * 8, toks), jnp.int32)],
        [x_got[0], x_first, *x_got[2:]],
        flops=2 * groups * slot_total * toks * width,
    )
    x_send, slots = got[:owners], got[owners]
    rows_x = [x_send[0]] + [swap(x_send[bits], bits) for bits in range(1, owners)]

    full = pl.BlockSpec(memory_space=pltpu.VMEM)
    piece = arr((block, units))
    piece_flops = 2 * block * units * width
    dispatch_flops = 2 * groups * slot_total * toks * width
    packed = arr((2, local, block, width))

    def pack_rows(out_ref, refs):
        for half in range(2):
            for i in range(local):
                for bits in range(owners):
                    at = slice(bits * pair_rows, (bits + 1) * pair_rows)
                    out_ref[half, i, at, :] = refs[bits][half, i]

    halves, experts = range(2), range(local)
    order = [(kind, half, i) for half in halves for i in experts for kind in "gu"]
    order += [("b", half, i) for half in halves for i in experts]
    weight_of = {"g": w_gate, "u": w_up, "b": w_down}
    part, pair, total, final, near, far = {}, {}, {}, {}, {}, {}

    def first_body(*refs):
        x_refs, w_refs = refs[:owners], refs[owners : owners + 2]
        d_refs, slot_ref = refs[owners + 2 : owners + 2 + groups], refs[owners + 2 + groups]
        outs = refs[owners + 3 + groups :]
        pack_rows(outs[2], x_refs)
        for out, w_ref in zip(outs[:2], w_refs):
            out[...] = mm(outs[2][0, 0], w_ref[0]).astype(BF16)
        for step in range(groups):
            group = group_at(-step)
            slot = slot_ref[pl.ds(group * 8, 8), :][0:1]
            send_rows(picker(slot), d_refs[step][...], group, outs[3:])

    got = call(
        first_body,
        [piece, piece, packed] + [message] * owners,
        [*rows_x, w_gate, w_up, *d_got, slots],
        flops=2 * piece_flops + dispatch_flops,
    )
    part[0], part[1], packed_x = got[:3]
    d_send = got[3:]
    near[0], near[1] = line_hop(part[0], inward), line_hop(part[1], inward)
    rows_d = [d_send[0]] + [swap(d_send[bits], bits) for bits in range(1, owners)]

    def at_end():
        place = lax.axis_index("dp")
        return (place == 0) | (place == groups - 1)

    def plus(left_ref, right_ref):
        return (left_ref[...].astype(F32) + right_ref[...].astype(F32)).astype(BF16)

    count = len(order)

    def slot_call(t, rows=None, unpacked=None):
        take, cross, done = t < count, 0 <= t - 2 < count, 0 <= t - 4 < count
        ahead = t + 2 < count
        ins, specs, outs = [near[t]], [full], []
        if take:
            ins.append(part[t])
            outs.append(piece)
        if cross:
            ins += [pair[t - 2], far[t - 2]]
            outs.append(piece)
        if done:
            ins.append(total[t - 4])
            outs.append(piece)
        specs = [full] * len(ins)
        if ahead:
            kind, half, i = order[t + 2]
            ins += [rows, weight_of[kind]]
            specs += [
                pl.BlockSpec((1, 1, block, width), lambda *_: (half, i, 0, 0)),
                pl.BlockSpec((1, *weight_of[kind].shape[1:]), lambda *_: (i, 0, 0)),
            ]
            outs.append(piece)
        if ahead and cross:
            outs.append(piece)
        if unpacked is not None:
            ins += unpacked
            specs += [full] * owners
            outs.append(packed)
        ins_count = len(ins)

        def body(*refs):
            left, right = list(refs[:ins_count]), list(refs[ins_count:])
            got_ref = left.pop(0)
            total_ref = None
            if take:
                right.pop(0)[...] = plus(left.pop(0), got_ref)
            if cross:
                total_ref = right.pop(0)
                total_ref[...] = plus(left.pop(0), left.pop(0))
            if done:
                right.pop(0)[...] = jnp.where(at_end(), got_ref[...], left.pop(0)[...])
            if ahead:
                rows_ref, w_ref, part_ref = left.pop(0), left.pop(0), right.pop(0)
                product = mm_nt if kind == "b" else mm
                part_ref[...] = product(rows_ref[0, 0], w_ref[0]).astype(BF16)
                if cross:
                    right.pop(0)[...] = jnp.where(at_end(), part_ref[...], total_ref[...])
            if unpacked is not None:
                pack_rows(right.pop(0), left)

        got = list(call(body, outs, ins, specs=specs, flops=piece_flops if ahead else 0))
        if take:
            pair[t] = got.pop(0)
            far[t] = line_hop(pair[t], [(1, 2), (2, 1)])
        if cross:
            total[t - 2] = got.pop(0)
        if done:
            final[order[t - 4]] = got.pop(0)
        if ahead:
            part[t + 2] = got.pop(0)
        if ahead and cross:
            near[t + 2] = line_hop(got.pop(0), inward + outward)
        elif ahead:
            near[t + 2] = line_hop(part[t + 2], inward)
        elif cross:
            near[t + 2] = line_hop(total[t - 2], outward)
        return got

    for t in range(3):
        slot_call(t, packed_x)
    (packed_d,) = slot_call(3, packed_x, unpacked=rows_d)
    for t in range(4, count):
        slot_call(t, packed_x if t + 2 < 2 * 2 * local else packed_d)

    def spread(refs, half, i, value):
        for bits in range(owners):
            rows = value[bits * pair_rows : (bits + 1) * pair_rows]
            if half is None:
                refs[bits][i] = rows
            else:
                refs[bits][half, i] = rows

    acts = arr((half_rows, units))

    def out_body(*refs):
        w_ref, outs = refs[4 * local], refs[4 * local + 1 :]
        hidden_refs, out_refs = outs[:2], outs[2:]
        for half in halves:
            for i in experts:
                at = 2 * (half * local + i)
                gate, up = refs[at][...].astype(F32), refs[at + 1][...].astype(F32)
                rows = (gate * jax.nn.sigmoid(gate) * up).astype(BF16)
                hidden_refs[half][i * block : (i + 1) * block, :] = rows
                spread(out_refs, half, i, mm(rows, w_ref[i]).astype(BF16))

    got = call(
        out_body,
        [acts, acts] + [message] * owners,
        [final[name] for name in order[: 4 * local]] + [w_down],
        flops=2 * local * piece_flops,
    )
    hidden, out_send = got[:2], got[2:]
    out_got = [out_send[0]] + [swap(out_send[bits], bits) for bits in range(1, owners)]

    for t in range(count, count + 4):
        slot_call(t)

    half_message = arr((local, pair_rows, width))

    def combined(slot_ref, group, block_of):
        place = group // 2 * cap
        rows = [
            block_of(bits, i, slice(place, place + cap))
            for bits in range(owners)
            for i in range(local)
        ]
        pick = picker(slot_ref[group * 8 : group * 8 + 1, :])
        return mm_tn(pick, jnp.concatenate(rows, axis=0)).astype(BF16)

    def in_call(half):
        ins = [final[kind, half, i] for i in experts for kind in "gub"] + [w_gate, w_up]
        count = len(ins)

        def body(*refs):
            gate_w, up_w = refs[count - 2], refs[count - 1]
            act_refs, in_refs = refs[count : count + 2], refs[count + 2 :]
            for i in experts:
                gate, up, grad = (refs[3 * i + n][...].astype(F32) for n in range(3))
                rows = slice(i * block, (i + 1) * block)
                sigma = jax.nn.sigmoid(gate)
                act_gate = (grad * up * sigma * (1.0 + gate * (1.0 - sigma))).astype(BF16)
                act_up = (grad * (gate * sigma)).astype(BF16)
                act_refs[0][rows, :] = act_gate
                act_refs[1][rows, :] = act_up
                into = mm_nt(act_gate, gate_w[i]) + mm_nt(act_up, up_w[i])
                spread(in_refs, None, i, into.astype(BF16))

        got = call(
            body, [acts, acts] + [half_message] * owners, ins, flops=4 * piece_flops
        )
        sent = got[2:]
        return got[:2], [sent[0]] + [swap(sent[bits], bits) for bits in range(1, owners)]

    acts0, in_got0 = in_call(0)
    acts1, in_got1 = in_call(1)

    def tokens_body(*refs):
        o_refs, i_refs, slot_ref = refs[:owners], refs[owners : 2 * owners], refs[2 * owners]
        outs = refs[2 * owners + 2 :]
        sum_ref = refs[-1]
        for group in range(groups):
            sum_ref[group] = combined(
                slot_ref, group, lambda bits, i, rows: o_refs[bits][group % 2, i, rows, :]
            )
        for group in range(0, groups, 2):
            outs[groups][group // 2] = combined(
                slot_ref, group, lambda bits, i, rows: i_refs[bits][i, rows, :]
            )
        for step in range(groups):
            outs[step][...] = sum_ref[group_at(-step)]

    got = call(
        tokens_body,
        [arr((toks, width))] * groups + [arr((groups // 2, toks, width))],
        [*out_got, *in_got0, slots, acts1[0]],
        scratch=[pltpu.VMEM((groups, toks, width), BF16)],
        flops=2 * dispatch_flops,
    )
    out_tok, in_even = got[:groups], got[groups]
    out_chunk = [out_tok[0]] + [shift(out_tok[step], -step) for step in range(1, groups)]

    def in_tokens_body(*refs):
        i_refs, even_ref, slot_ref = refs[:owners], refs[owners], refs[owners + 1]
        sum_ref = refs[-1]
        for group in range(groups):
            if group % 2 == 0:
                sum_ref[group] = even_ref[group // 2]
            else:
                sum_ref[group] = combined(
                    slot_ref, group, lambda bits, i, rows: i_refs[bits][i, rows, :]
                )
        for step in range(groups):
            refs[owners + 2 + step][...] = sum_ref[group_at(-step)]

    in_tok = call(
        in_tokens_body,
        [arr((toks, width))] * groups,
        [*in_got1, in_even, slots],
        scratch=[pltpu.VMEM((groups, toks, width), BF16)],
        flops=dispatch_flops,
    )
    in_chunk = [in_tok[0]] + [shift(in_tok[step], -step) for step in range(1, groups)]

    per_part = groups // 2
    part_width = per_part * width

    def assemble_body(*refs):
        chunk_refs, give_ref, keep_ref, whole_ref = refs[:groups], *refs[groups:]
        for step in range(groups):
            whole_ref[group_at(step)] = chunk_refs[step][...]
        mine = lax.axis_index("tensor")
        for j in range(per_part):
            at = slice(j * width, (j + 1) * width)
            give_ref[:, at] = whole_ref[(1 - mine) * per_part + j]
            keep_ref[:, at] = whole_ref[mine * per_part + j]

    def assemble(chunks):
        give, keep = call(
            assemble_body,
            [arr((toks, part_width))] * 2,
            chunks,
            scratch=[pltpu.VMEM((groups, toks, width), BF16)],
        )
        other = lax.ppermute(give, "tensor", [(0, 1), (1, 0)])
        return keep.astype(F32) + other.astype(F32)

    output = (mix_wide[:, 0:1] * assemble(out_chunk)).astype(BF16)
    grad_tokens = assemble(in_chunk).astype(BF16)

    def weight_grad(rows, acts, shape, rows_first):
        def body(*refs):
            for i in range(local):
                part_sum = None
                for half in range(2):
                    left, right = refs[0][half, i], refs[1 + half][i * block : (i + 1) * block, :]
                    if not rows_first:
                        left, right = right, left
                    term = mm_tn(left, right)
                    part_sum = term if part_sum is None else part_sum + term
                refs[-1][i] = part_sum

        return call(body, [arr(shape, F32)], [rows, *acts], flops=4 * piece_flops)[0]

    grad_gate = weight_grad(packed_x, [acts0[0], acts1[0]], w_gate.shape, True)
    grad_up = weight_grad(packed_x, [acts0[1], acts1[1]], w_up.shape, True)
    grad_down = weight_grad(packed_d, hidden, w_down.shape, False)
    return (output, grad_tokens, grad_gate, grad_up, grad_down)


def on_device(tokens, cotangent, scores, routes, w_gate, w_up, w_down):
    owners = lax.axis_size("expert")
    toks = tokens.shape[0]
    cap = min(toks, 2 * toks // (w_gate.shape[0] * owners))
    held = w_gate.shape[0] * cap
    fits = (
        lax.axis_size("dp") == 4
        and lax.axis_size("tensor") == 2
        and owners == 4
        and cap % 16 == 0
        and held & (held - 1) == 0
        and toks == 128
        and w_gate.shape[1] % 128 == 0
        and w_gate.shape[2] % 128 == 0
    )
    form = kernel_form if fits else plain_form
    return form(tokens, cotangent, scores, routes, w_gate, w_up, w_down)


def solution(mesh):
    in_specs = (
        P(("dp", "expert"), None),
        P(("dp", "expert"), None),
        P(("dp", "expert"), None),
        P(("dp", "expert"), None),
        P("expert", "dp", "tensor"),
        P("expert", "dp", "tensor"),
        P("expert", "tensor", "dp"),
    )
    out_specs = (
        P(("dp", "expert"), "tensor"),
        P(("dp", "expert"), "tensor"),
        P("expert", "dp", "tensor"),
        P("expert", "dp", "tensor"),
        P("expert", "tensor", "dp"),
    )
    return jax.shard_map(
        on_device, mesh=mesh, in_specs=in_specs, out_specs=out_specs, check_vma=False
    )
```

```python
import jax
import jax.numpy as jnp
from jax import lax
from jax.experimental import pallas as pl
from jax.experimental.pallas import tpu as pltpu
from jax.sharding import PartitionSpec as P

F32 = jnp.float32
BF16 = jnp.bfloat16


def dot(eq, a, b):
    return jnp.einsum(eq, a, b, preferred_element_type=F32)


def plain_form(tokens, cotangent, scores, routes, w_gate, w_up, w_down):
    tok_count, model_width = tokens.shape
    owners = lax.axis_size("expert")
    groups = lax.axis_size("dp")
    sharers = lax.axis_size("tensor")
    local_count = w_gate.shape[0]
    expert_count = local_count * owners
    capacity = min(tok_count, 2 * tok_count // expert_count)
    held = local_count * capacity
    width = model_width // groups
    my_group = lax.axis_index("dp")
    my_owner = lax.axis_index("expert")
    my_part = lax.axis_index("tensor")

    def shift(value, step):
        if step % groups == 0:
            return value
        return lax.ppermute(value, "dp", [(j, (j + step) % groups) for j in range(groups)])

    def swap(value, bits):
        if bits == 0:
            return value
        return lax.ppermute(value, "expert", [(j, j ^ bits) for j in range(owners)])

    def chunks_out(rows):
        parts = []
        for step in range(groups):
            start = lax.rem(my_group + step, groups) * width
            parts.append(shift(lax.dynamic_slice(rows, (0, start), (tok_count, width)), step))
        return parts

    def picked(stack, index):
        return lax.dynamic_index_in_dim(stack, lax.rem(index + groups, groups), 0, keepdims=False)

    def by_group(parts):
        stack = jnp.stack(parts)
        return jnp.stack([picked(stack, my_group - g) for g in range(groups)])

    routes_all = by_group([shift(routes[:, 0], step) for step in range(groups)])
    x_chunk = by_group(chunks_out(tokens))
    mix = scores[:, :1] / jnp.sum(scores, axis=1, keepdims=True)
    weighted = (mix * cotangent.astype(F32)).astype(BF16)
    d_chunk = by_group(chunks_out(weighted))

    member = (routes_all[:, :, None] == jnp.arange(expert_count, dtype=jnp.int32)).astype(F32)
    earlier = jnp.tril(jnp.ones((tok_count, tok_count), BF16), -1)
    before = dot("ab,gbe->gae", earlier, member.astype(BF16))
    place = jnp.sum(before * member, axis=2).astype(jnp.int32)
    slot_ids = routes_all * capacity + place

    def picker(bits):
        base = (my_owner ^ bits) * held
        wanted = base + jnp.arange(held, dtype=jnp.int32).reshape(local_count, 1, capacity, 1)
        return (slot_ids[None, :, None, :] == wanted).astype(BF16)

    pickers = [picker(bits) for bits in range(owners)]

    def dispatch(chunk):
        got = []
        for bits in range(owners):
            send = dot("igct,gtk->igck", pickers[bits], chunk).astype(BF16)
            got.append(swap(send.reshape(local_count, groups * capacity, width), bits))
        return [jnp.concatenate([g[i] for g in got], axis=0) for i in range(local_count)]

    rows_x = dispatch(x_chunk)
    rows_d = dispatch(d_chunk)

    def line_sum(part):
        part = part.astype(BF16)
        if groups != 4:
            return lax.psum(part, "dp").astype(F32)
        near = lax.ppermute(part, "dp", [(0, 1), (3, 2)])
        pair = part.astype(F32) + near.astype(F32)
        far = lax.ppermute(pair.astype(BF16), "dp", [(1, 2), (2, 1)])
        total = (pair + far.astype(F32)).astype(BF16)
        back = lax.ppermute(total, "dp", [(1, 0), (2, 3)])
        at_end = (my_group == 0) | (my_group == groups - 1)
        return jnp.where(at_end, back, total).astype(F32)

    experts = range(local_count)
    gate_act, up_act, back_grad = {}, {}, {}
    for i in experts:
        gate_act[i] = line_sum(dot("rk,kf->rf", rows_x[i], w_gate[i]))
        up_act[i] = line_sum(dot("rk,kf->rf", rows_x[i], w_up[i]))
    for i in experts:
        back_grad[i] = line_sum(dot("rk,fk->rf", rows_d[i], w_down[i]))

    part_out, part_in, grad_gate, grad_up, grad_down = [], [], [], [], []
    for i in experts:
        sigma = jax.nn.sigmoid(gate_act[i])
        silu_act = gate_act[i] * sigma
        hidden = (silu_act * up_act[i]).astype(BF16)
        act_gate = (
            back_grad[i] * up_act[i] * sigma * (1.0 + gate_act[i] * (1.0 - sigma))
        ).astype(BF16)
        act_up = (back_grad[i] * silu_act).astype(BF16)
        part_out.append(dot("rf,fk->rk", hidden, w_down[i]).astype(BF16))
        into = dot("rf,kf->rk", act_gate, w_gate[i]) + dot("rf,kf->rk", act_up, w_up[i])
        part_in.append(into.astype(BF16))
        grad_gate.append(dot("rk,rf->kf", rows_x[i], act_gate))
        grad_up.append(dot("rk,rf->kf", rows_x[i], act_up))
        grad_down.append(dot("rf,rk->fk", hidden, rows_d[i]))

    pick_all = jnp.stack(pickers)

    def combine(parts):
        rows = jnp.stack(parts).reshape(local_count, owners, groups, capacity, width)
        back = jnp.stack([swap(rows[:, bits], bits) for bits in range(owners)])
        sums = dot("bigct,bigck->gtk", pick_all, back).astype(BF16)
        mine = jnp.stack(
            [shift(picked(sums, my_group - step), -step) for step in range(groups)]
        )
        whole = jnp.concatenate([picked(mine, c - my_group) for c in range(groups)], axis=1)
        if sharers != 2:
            return lax.psum_scatter(whole, "tensor", scatter_dimension=1, tiled=True).astype(F32)
        half = model_width // 2
        give = lax.dynamic_slice(whole, (0, (1 - my_part) * half), (tok_count, half))
        keep = lax.dynamic_slice(whole, (0, my_part * half), (tok_count, half))
        return keep.astype(F32) + lax.ppermute(give, "tensor", [(0, 1), (1, 0)]).astype(F32)

    output = (mix * combine(part_out)).astype(BF16)
    grad_tokens = combine(part_in).astype(BF16)
    return (output, grad_tokens, jnp.stack(grad_gate), jnp.stack(grad_up), jnp.stack(grad_down))


VMEM_LIMIT = 48 * 1024 * 1024


def call(body, outs, ins, scratch=(), flops=0, specs=None):
    moved = sum(a.size * a.dtype.itemsize for a in ins)
    moved += sum(o.size * o.dtype.itemsize for o in outs)
    many = pl.BlockSpec(memory_space=pltpu.VMEM)
    return pl.pallas_call(
        body,
        out_shape=outs,
        grid=() if specs is None else (1,),
        in_specs=[many] * len(ins) if specs is None else specs,
        out_specs=[many] * len(outs),
        scratch_shapes=list(scratch),
        compiler_params=pltpu.CompilerParams(vmem_limit_bytes=VMEM_LIMIT),
        cost_estimate=pl.CostEstimate(flops=flops, bytes_accessed=moved, transcendentals=0),
    )(*ins)


def arr(shape, dtype=BF16):
    return jax.ShapeDtypeStruct(shape, dtype)


def mm(a, b):
    return jnp.dot(a, b, preferred_element_type=F32)


def mm_nt(a, b):
    return lax.dot_general(a, b, (((1,), (1,)), ((), ())), preferred_element_type=F32)


def mm_tn(a, b):
    return lax.dot_general(a, b, (((0,), (0,)), ((), ())), preferred_element_type=F32)


def kernel_form(tokens, cotangent, scores, routes, w_gate, w_up, w_down):
    toks, model_width = tokens.shape
    owners, groups = lax.axis_size("expert"), lax.axis_size("dp")
    local, width, units = w_gate.shape
    expert_count = local * owners
    cap = min(toks, 2 * toks // expert_count)
    held = local * cap
    slot_total = expert_count * cap
    pair_rows = groups // 2 * cap
    half_rows = local * owners * pair_rows
    block = owners * pair_rows
    extra = 16

    def shift(value, step):
        return lax.ppermute(value, "dp", [(j, (j + step) % groups) for j in range(groups)])

    def swap(value, bits):
        return lax.ppermute(value, "expert", [(j, j ^ bits) for j in range(owners)])

    inward, outward = [(0, 1), (3, 2)], [(1, 0), (2, 3)]

    def line_hop(value, pairs):
        return lax.ppermute(value, "dp", pairs)

    def group_at(step):
        return lax.rem(lax.axis_index("dp") + step + groups, groups)

    def columns_at(step):
        return pl.ds(pl.multiple_of(group_at(step) * width, width), width)

    def pack_body(tok_ref, route_ref, *out_refs):
        row = lax.broadcasted_iota(jnp.int32, (extra, toks), 0)
        line = jnp.broadcast_to(route_ref[...].astype(F32), (extra, toks))
        line = jnp.where(row == 0, line, 0.0).astype(BF16)
        for step in range(groups):
            out = out_refs[step]
            out[0:toks, :] = tok_ref[:, columns_at(step)]
            out[toks : toks + extra, :] = jnp.zeros((extra, width), BF16)
            out[toks : toks + extra, 0:toks] = line

    x_pack = call(
        pack_body, [arr((toks + extra, width))] * groups, [tokens, routes.reshape(1, toks)]
    )
    x_got = [x_pack[0]] + [shift(x_pack[step], step) for step in range(1, groups)]

    def slots_row(line):
        first = lax.broadcasted_iota(jnp.int32, (toks, toks), 0)
        second = lax.broadcasted_iota(jnp.int32, (toks, toks), 1)
        whole = jnp.broadcast_to(line, (toks, toks))
        column = jnp.sum(jnp.where(first == second, whole, 0.0), axis=1, keepdims=True)
        same = (column == whole) & (first < second)
        place = jnp.sum(jnp.where(same, 1.0, 0.0), axis=0, keepdims=True)
        slot = (line * float(cap) + place).astype(jnp.int32)
        return slot ^ (lax.axis_index("expert") * held)

    def picker(slot):
        row = lax.broadcasted_iota(jnp.int32, (slot_total, toks), 0)
        return jnp.where(row == jnp.broadcast_to(slot, (slot_total, toks)), 1.0, 0.0).astype(BF16)

    def send_rows(pick, rows, group, out_refs):
        sent = mm(pick, rows).astype(BF16)
        parity, place = lax.rem(group, 2), lax.div(group, 2)
        rows_at = pl.ds(pl.multiple_of(place * cap, cap), cap)
        for bits in range(owners):
            for i in range(local):
                at = bits * held + i * cap
                out_refs[bits][parity, i, rows_at, :] = sent[at : at + cap]

    message = arr((2, local, pair_rows, width))

    def weigh_body(cot_ref, score_ref, weighted_ref, mix_ref):
        score = score_ref[...]
        mix = score[:, 0:1] / jnp.sum(score, axis=1, keepdims=True)
        mix_ref[...] = jnp.broadcast_to(mix, mix_ref.shape)
        weighted_ref[...] = (mix * cot_ref[...].astype(F32)).astype(BF16)

    weighted, mix_wide = call(
        weigh_body, [arr((toks, model_width)), arr((toks, 128), F32)], [cotangent, scores]
    )

    def dispatch_x_body(*refs):
        x_refs, weighted_ref, outs = refs[:groups], refs[groups], refs[groups + 1 :]
        send_refs, slot_ref, d_refs = outs[:owners], outs[owners], outs[owners + 1 :]
        for step in range(groups):
            group = group_at(-step)
            slot = slots_row(x_refs[step][toks : toks + extra, 0:toks][0:1].astype(F32))
            slot_ref[pl.ds(group * 8, 8), :] = jnp.broadcast_to(slot, (8, toks))
            send_rows(picker(slot), x_refs[step][0:toks, :], group, send_refs)
            d_refs[step][...] = weighted_ref[:, columns_at(step)]

    got = call(
        dispatch_x_body,
        [message] * owners + [arr((groups * 8, toks), jnp.int32)] + [arr((toks, width))] * groups,
        [*x_got, weighted],
        flops=2 * groups * slot_total * toks * width,
    )
    x_send, slots, d_pack = got[:owners], got[owners], got[owners + 1 :]
    d_got = [d_pack[0]] + [shift(d_pack[step], step) for step in range(1, groups)]
    rows_x = [x_send[0]] + [swap(x_send[bits], bits) for bits in range(1, owners)]

    full = pl.BlockSpec(memory_space=pltpu.VMEM)
    piece = arr((block, units))
    piece_flops = 2 * block * units * width
    dispatch_flops = 2 * groups * slot_total * toks * width
    packed = arr((2, local, block, width))

    def pack_rows(out_ref, refs):
        for half in range(2):
            for i in range(local):
                for bits in range(owners):
                    at = slice(bits * pair_rows, (bits + 1) * pair_rows)
                    out_ref[half, i, at, :] = refs[bits][half, i]

    halves, experts = range(2), range(local)
    assert local == 2
    order = [(kind, 0, i) for i in experts for kind in "gu"]
    order += [("g", 1, 0), ("u", 1, 0), ("b", 0, 0), ("b", 0, 1)]
    order += [("g", 1, 1), ("u", 1, 1), ("b", 1, 0), ("b", 1, 1)]
    weight_of = {"g": w_gate, "u": w_up, "b": w_down}
    part, pair, total, final, near, far = {}, {}, {}, {}, {}, {}

    def first_body(*refs):
        x_refs, w_refs, outs = refs[:owners], refs[owners : owners + 2], refs[owners + 4 :]
        outs[3][...], outs[4][...] = refs[owners + 2][...], refs[owners + 3][...]
        pack_rows(outs[2], x_refs)
        for out, w_ref in zip(outs[:2], w_refs):
            out[...] = mm(outs[2][0, 0], w_ref[0]).astype(BF16)

    part[0], part[1], packed_x, d_got[1], d_got[3] = call(
        first_body,
        [piece, piece, packed] + [arr((toks, width))] * 2,
        [*rows_x, w_gate, w_up, d_got[1], d_got[3]],
        flops=2 * piece_flops,
    )
    near[0], near[1] = line_hop(part[0], inward), line_hop(part[1], inward)

    def dispatch_d_body(*refs):
        d_refs, slot_ref, out_refs = refs[:groups], refs[groups], refs[groups + 1 :]
        for step in range(groups):
            group = group_at(-step)
            slot = slot_ref[pl.ds(group * 8, 8), :][0:1]
            send_rows(picker(slot), d_refs[step][...], group, out_refs)

    def at_end():
        place = lax.axis_index("dp")
        return (place == 0) | (place == groups - 1)

    def plus(left_ref, right_ref):
        return (left_ref[...].astype(F32) + right_ref[...].astype(F32)).astype(BF16)

    count = len(order)

    def slot_call(t, unpacked=None, also=None):
        take, cross, done = t < count, 0 <= t - 2 < count, 0 <= t - 4 < count
        ahead = t + 2 < count
        ins, specs, outs = [near[t]], [full], []
        if take:
            ins.append(part[t])
            outs.append(piece)
        if cross:
            ins += [pair[t - 2], far[t - 2]]
            outs.append(piece)
        if done:
            ins.append(total[t - 4])
            outs.append(piece)
        specs = [full] * len(ins)
        if ahead:
            kind, half, i = order[t + 2]
            ins += [packed_d if kind == "b" else packed_x, weight_of[kind]]
            specs += [
                pl.BlockSpec((1, 1, block, width), lambda *_: (half, i, 0, 0)),
                pl.BlockSpec((1, *weight_of[kind].shape[1:]), lambda *_: (i, 0, 0)),
            ]
            outs.append(piece)
        if ahead and cross:
            outs.append(piece)
        if unpacked is not None:
            ins += unpacked
            specs += [full] * owners
            outs.append(packed)
        if also is not None:
            ins += also[1]
            specs += [full] * len(also[1])
            outs += also[2]
        ins_count = len(ins)

        def body(*refs):
            left, right = list(refs[:ins_count]), list(refs[ins_count:])
            got_ref = left.pop(0)
            total_ref = None
            if take:
                right.pop(0)[...] = plus(left.pop(0), got_ref)
            if cross:
                total_ref = right.pop(0)
                total_ref[...] = plus(left.pop(0), left.pop(0))
            if done:
                final_ref = right.pop(0)
                final_ref[...] = jnp.where(at_end(), got_ref[...], left.pop(0)[...])
            if ahead:
                rows_ref, w_ref, part_ref = left.pop(0), left.pop(0), right.pop(0)
                product = mm_nt if kind == "b" else mm
                part_ref[...] = product(rows_ref[0, 0], w_ref[0]).astype(BF16)
                if cross:
                    right.pop(0)[...] = jnp.where(at_end(), part_ref[...], total_ref[...])
            if unpacked is not None:
                pack_rows(right.pop(0), left)
            if also is not None:
                also[0](*left, *right, *([total_ref, final_ref] if done else []))

        got = list(call(body, outs, ins, specs=specs, flops=piece_flops if ahead else 0))
        if take:
            pair[t] = got.pop(0)
            far[t] = line_hop(pair[t], [(1, 2), (2, 1)])
        if cross:
            total[t - 2] = got.pop(0)
        if done:
            final[order[t - 4]] = got.pop(0)
        if ahead:
            part[t + 2] = got.pop(0)
        if ahead and cross:
            near[t + 2] = line_hop(got.pop(0), inward + outward)
        elif ahead:
            near[t + 2] = line_hop(part[t + 2], inward)
        return got

    d_send = slot_call(0, also=(dispatch_d_body, [*d_got, slots], [message] * owners))
    rows_d = [d_send[0]] + [swap(d_send[bits], bits) for bits in range(1, owners)]
    slot_call(1)
    slot_call(2)
    (packed_d,) = slot_call(3, unpacked=rows_d)
    for t in range(4, 7):
        slot_call(t)

    acts, half_message = arr((half_rows, units)), arr((local, pair_rows, width))

    def spread(refs, i, value):
        for bits in range(owners):
            refs[bits][i] = value[bits * pair_rows : (bits + 1) * pair_rows]

    assert local == 2
    acts, two_pieces = arr((half_rows, units)), arr((2, block, units))

    def out_rows(refs, w_ref, hidden_ref, out_refs):
        for i in experts:
            gate, up = refs[2 * i][...].astype(F32), refs[2 * i + 1][...].astype(F32)
            rows = (gate * jax.nn.sigmoid(gate) * up).astype(BF16)
            hidden_ref[i * block : (i + 1) * block, :] = rows
            spread(out_refs, i, mm(rows, w_ref[i]).astype(BF16))

    def even_out_body(*refs):
        known, (w_ref, hidden_ref), out_refs = refs[:3], refs[3:5], refs[5 : 5 + owners]
        out_rows([*known, refs[-1]], w_ref, hidden_ref, out_refs)

    def sent_over(messages):
        return [messages[0]] + [swap(messages[bits], bits) for bits in range(1, owners)]

    def several(refs, *counts):
        taken, at = [], 0
        for n in counts:
            taken.append(refs[at : at + n])
            at += n
        return taken

    def chosen(total_piece, back_piece):
        return jnp.where(at_end(), back_piece, total_piece)

    def into_rows(gu, grads, w_refs, act_refs, in_refs):
        for i in experts:
            gate, up, grad = (v.astype(F32) for v in (gu[2 * i], gu[2 * i + 1], grads[i]))
            rows = slice(i * block, (i + 1) * block)
            sigma = jax.nn.sigmoid(gate)
            act_gate = (grad * up * sigma * (1.0 + gate * (1.0 - sigma))).astype(BF16)
            act_up = (grad * (gate * sigma)).astype(BF16)
            act_refs[0][rows, :] = act_gate
            act_refs[1][rows, :] = act_up
            into = mm_nt(act_gate, w_refs[0][i]) + mm_nt(act_up, w_refs[1][i])
            spread(in_refs, i, into.astype(BF16))

    assert count == 12
    got = slot_call(
        7,
        also=(
            even_out_body,
            [final[name] for name in order[:3]] + [w_down],
            [acts] + [half_message] * owners,
        ),
    )
    hidden_even, out_even = got[0], sent_over(got[1:])
    for t in range(8, 10):
        slot_call(t)
    slot_call(10, also=(lambda *refs: None, out_even[1:], []))

    two_pieces = arr((2, block, units))
    even_names = [name for name in order[:4]]

    def in_even_body(*refs):
        known, (b_ref, before_ref), w_refs, act_refs, in_refs, (two_ref, total_ref, final_ref) = (
            several(refs, 4, 2, 2, 2, owners, 3)
        )
        two_ref[0], two_ref[1] = before_ref[...], total_ref[...]
        grads = [b_ref[...], final_ref[...]]
        into_rows([r[...] for r in known], grads, w_refs, act_refs, in_refs)

    got = slot_call(
        11,
        also=(
            in_even_body,
            [final[name] for name in even_names] + [final["b", 0, 0], total[8], w_gate, w_up],
            [acts, acts] + [half_message] * owners + [two_pieces],
        ),
    )
    acts0, in_got0, two_total = got[:2], sent_over(got[2:-1]), got[-1]
    two_back = line_hop(two_total, outward)

    def cross_body(*refs):
        for n in range(2):
            refs[4][n] = plus(refs[2 * n], refs[2 * n + 1])

    (odd_total,) = call(cross_body, [two_pieces], [pair[10], far[10], pair[11], far[11]])
    odd_back = line_hop(odd_total, outward)

    def odd_out_body(*refs):
        known, (total_ref, back_ref, w_ref, hidden_ref), out_refs, last_refs = several(
            refs, 2, 4, owners, 2
        )
        for n in range(2):
            last_refs[n][...] = chosen(total_ref[n], back_ref[n])
        out_rows([*known, *last_refs], w_ref, hidden_ref, out_refs)

    got = call(
        odd_out_body,
        [acts] + [half_message] * owners + [piece] * 2,
        [final["g", 1, 0], final["u", 1, 0], two_total, two_back, w_down],
        flops=2 * local * piece_flops,
    )
    hidden, out_odd, gu_last = [hidden_even, got[0]], sent_over(got[1:-2]), got[-2:]

    def last_body(*refs):
        known, (total_ref, back_ref), w_refs, _, act_refs, in_refs = several(
            refs, 4, 2, 2, owners, 2, owners
        )
        grads = [chosen(total_ref[i], back_ref[i]) for i in experts]
        into_rows([r[...] for r in known], grads, w_refs, act_refs, in_refs)

    got = call(
        last_body,
        [acts, acts] + [half_message] * owners,
        [final["g", 1, 0], final["u", 1, 0], *gu_last, odd_total, odd_back, w_gate, w_up]
        + [*in_got0[1:], out_odd[1]],
        flops=4 * local * piece_flops,
    )
    acts1, in_got1 = got[:2], sent_over(got[2:])

    def combined(slot_ref, group, block_of):
        place = group // 2 * cap
        rows = [
            block_of(bits, i, slice(place, place + cap))
            for bits in range(owners)
            for i in range(local)
        ]
        pick = picker(slot_ref[group * 8 : group * 8 + 1, :])
        return mm_tn(pick, jnp.concatenate(rows, axis=0)).astype(BF16)

    def out_tokens_body(*refs):
        even_refs, odd_refs, (slot_ref, _), tok_refs, (sum_ref,) = several(
            refs, owners, owners, 2, groups, 1
        )
        for group in range(groups):
            o_refs = odd_refs if group % 2 else even_refs
            sum_ref[group] = combined(
                slot_ref, group, lambda bits, i, rows: o_refs[bits][i, rows, :]
            )
        for step in range(groups):
            tok_refs[step][...] = sum_ref[group_at(-step)]

    whole_rows = [pltpu.VMEM((groups, toks, width), BF16)]
    out_tok = call(
        out_tokens_body,
        [arr((toks, width))] * groups,
        [*out_even, *out_odd, slots, acts1[0]],
        scratch=whole_rows,
        flops=dispatch_flops,
    )
    out_chunk = [out_tok[0]] + [shift(out_tok[step], -step) for step in range(1, groups)]

    def in_tokens_body(*refs):
        even_refs, odd_refs, (slot_ref,), tok_refs, (sum_ref,) = several(
            refs, owners, owners, 1, groups, 1
        )
        for group in range(groups):
            i_refs = odd_refs if group % 2 else even_refs
            sum_ref[group] = combined(
                slot_ref, group, lambda bits, i, rows: i_refs[bits][i, rows, :]
            )
        for step in range(groups):
            tok_refs[step][...] = sum_ref[group_at(-step)]

    in_tok = call(
        in_tokens_body,
        [arr((toks, width))] * groups,
        [*in_got0, *in_got1, slots],
        scratch=whole_rows,
        flops=dispatch_flops,
    )
    in_chunk = [in_tok[0]] + [shift(in_tok[step], -step) for step in range(1, groups)]

    per_part = groups // 2

    def assemble_body(*refs):
        chunk_refs, (give_ref, keep_ref, whole_ref) = several(refs, groups, 3)
        for step in range(groups):
            whole_ref[group_at(step)] = chunk_refs[step][...]
        mine = lax.axis_index("tensor")
        for j in range(per_part):
            at = slice(j * width, (j + 1) * width)
            give_ref[:, at] = whole_ref[(1 - mine) * per_part + j]
            keep_ref[:, at] = whole_ref[mine * per_part + j]

    def across(chunks):
        give, keep = call(
            assemble_body, [arr((toks, per_part * width))] * 2, chunks, scratch=whole_rows
        )
        other = lax.ppermute(give, "tensor", [(0, 1), (1, 0)])
        return keep.astype(F32) + other.astype(F32)

    output = (mix_wide[:, 0:1] * across(out_chunk)).astype(BF16)
    grad_tokens = across(in_chunk).astype(BF16)

    def weight_grad(rows, acts, shape, rows_first):
        def body(*refs):
            for i in range(local):
                part_sum = None
                for half in range(2):
                    left, right = refs[0][half, i], refs[1 + half][i * block : (i + 1) * block, :]
                    if not rows_first:
                        left, right = right, left
                    term = mm_tn(left, right)
                    part_sum = term if part_sum is None else part_sum + term
                refs[-1][i] = part_sum

        return call(body, [arr(shape, F32)], [rows, *acts], flops=4 * piece_flops)[0]

    grad_gate = weight_grad(packed_x, [acts0[0], acts1[0]], w_gate.shape, True)
    grad_up = weight_grad(packed_x, [acts0[1], acts1[1]], w_up.shape, True)
    grad_down = weight_grad(packed_d, hidden, w_down.shape, False)
    return (output, grad_tokens, grad_gate, grad_up, grad_down)


def on_device(tokens, cotangent, scores, routes, w_gate, w_up, w_down):
    owners = lax.axis_size("expert")
    toks = tokens.shape[0]
    cap = min(toks, 2 * toks // (w_gate.shape[0] * owners))
    held = w_gate.shape[0] * cap
    fits = (
        lax.axis_size("dp") == 4
        and lax.axis_size("tensor") == 2
        and owners == 4
        and cap % 16 == 0
        and held & (held - 1) == 0
        and toks == 128
        and w_gate.shape[1] % 128 == 0
        and w_gate.shape[2] % 128 == 0
    )
    form = kernel_form if fits else plain_form
    return form(tokens, cotangent, scores, routes, w_gate, w_up, w_down)


def solution(mesh):
    in_specs = (
        P(("dp", "expert"), None),
        P(("dp", "expert"), None),
        P(("dp", "expert"), None),
        P(("dp", "expert"), None),
        P("expert", "dp", "tensor"),
        P("expert", "dp", "tensor"),
        P("expert", "tensor", "dp"),
    )
    out_specs = (
        P(("dp", "expert"), "tensor"),
        P(("dp", "expert"), "tensor"),
        P("expert", "dp", "tensor"),
        P("expert", "dp", "tensor"),
        P("expert", "tensor", "dp"),
    )
    return jax.shard_map(
        on_device, mesh=mesh, in_specs=in_specs, out_specs=out_specs, check_vma=False
    )
```

```python
import jax
import jax.numpy as jnp
from jax import lax
from jax.experimental import pallas as pl
from jax.experimental.pallas import tpu as pltpu
from jax.sharding import PartitionSpec as P

F32 = jnp.float32
BF16 = jnp.bfloat16


def dot(eq, a, b):
    return jnp.einsum(eq, a, b, preferred_element_type=F32)


def plain_form(tokens, cotangent, scores, routes, w_gate, w_up, w_down):
    tok_count, model_width = tokens.shape
    owners = lax.axis_size("expert")
    groups = lax.axis_size("dp")
    sharers = lax.axis_size("tensor")
    local_count = w_gate.shape[0]
    expert_count = local_count * owners
    capacity = min(tok_count, 2 * tok_count // expert_count)
    held = local_count * capacity
    width = model_width // groups
    my_group = lax.axis_index("dp")
    my_owner = lax.axis_index("expert")
    my_part = lax.axis_index("tensor")

    def shift(value, step):
        if step % groups == 0:
            return value
        return lax.ppermute(value, "dp", [(j, (j + step) % groups) for j in range(groups)])

    def swap(value, bits):
        if bits == 0:
            return value
        return lax.ppermute(value, "expert", [(j, j ^ bits) for j in range(owners)])

    def chunks_out(rows):
        parts = []
        for step in range(groups):
            start = lax.rem(my_group + step, groups) * width
            parts.append(shift(lax.dynamic_slice(rows, (0, start), (tok_count, width)), step))
        return parts

    def picked(stack, index):
        return lax.dynamic_index_in_dim(stack, lax.rem(index + groups, groups), 0, keepdims=False)

    def by_group(parts):
        stack = jnp.stack(parts)
        return jnp.stack([picked(stack, my_group - g) for g in range(groups)])

    routes_all = by_group([shift(routes[:, 0], step) for step in range(groups)])
    x_chunk = by_group(chunks_out(tokens))
    mix = scores[:, :1] / jnp.sum(scores, axis=1, keepdims=True)
    weighted = (mix * cotangent.astype(F32)).astype(BF16)
    d_chunk = by_group(chunks_out(weighted))

    member = (routes_all[:, :, None] == jnp.arange(expert_count, dtype=jnp.int32)).astype(F32)
    earlier = jnp.tril(jnp.ones((tok_count, tok_count), BF16), -1)
    before = dot("ab,gbe->gae", earlier, member.astype(BF16))
    place = jnp.sum(before * member, axis=2).astype(jnp.int32)
    slot_ids = routes_all * capacity + place

    def picker(bits):
        base = (my_owner ^ bits) * held
        wanted = base + jnp.arange(held, dtype=jnp.int32).reshape(local_count, 1, capacity, 1)
        return (slot_ids[None, :, None, :] == wanted).astype(BF16)

    pickers = [picker(bits) for bits in range(owners)]

    def dispatch(chunk):
        got = []
        for bits in range(owners):
            send = dot("igct,gtk->igck", pickers[bits], chunk).astype(BF16)
            got.append(swap(send.reshape(local_count, groups * capacity, width), bits))
        return [jnp.concatenate([g[i] for g in got], axis=0) for i in range(local_count)]

    rows_x = dispatch(x_chunk)
    rows_d = dispatch(d_chunk)

    def line_sum(part):
        part = part.astype(BF16)
        if groups != 4:
            return lax.psum(part, "dp").astype(F32)
        near = lax.ppermute(part, "dp", [(0, 1), (3, 2)])
        pair = part.astype(F32) + near.astype(F32)
        far = lax.ppermute(pair.astype(BF16), "dp", [(1, 2), (2, 1)])
        total = (pair + far.astype(F32)).astype(BF16)
        back = lax.ppermute(total, "dp", [(1, 0), (2, 3)])
        at_end = (my_group == 0) | (my_group == groups - 1)
        return jnp.where(at_end, back, total).astype(F32)

    experts = range(local_count)
    gate_act, up_act, back_grad = {}, {}, {}
    for i in experts:
        gate_act[i] = line_sum(dot("rk,kf->rf", rows_x[i], w_gate[i]))
        up_act[i] = line_sum(dot("rk,kf->rf", rows_x[i], w_up[i]))
    for i in experts:
        back_grad[i] = line_sum(dot("rk,fk->rf", rows_d[i], w_down[i]))

    part_out, part_in, grad_gate, grad_up, grad_down = [], [], [], [], []
    for i in experts:
        sigma = jax.nn.sigmoid(gate_act[i])
        silu_act = gate_act[i] * sigma
        hidden = (silu_act * up_act[i]).astype(BF16)
        act_gate = (
            back_grad[i] * up_act[i] * sigma * (1.0 + gate_act[i] * (1.0 - sigma))
        ).astype(BF16)
        act_up = (back_grad[i] * silu_act).astype(BF16)
        part_out.append(dot("rf,fk->rk", hidden, w_down[i]).astype(BF16))
        into = dot("rf,kf->rk", act_gate, w_gate[i]) + dot("rf,kf->rk", act_up, w_up[i])
        part_in.append(into.astype(BF16))
        grad_gate.append(dot("rk,rf->kf", rows_x[i], act_gate))
        grad_up.append(dot("rk,rf->kf", rows_x[i], act_up))
        grad_down.append(dot("rf,rk->fk", hidden, rows_d[i]))

    pick_all = jnp.stack(pickers)

    def combine(parts):
        rows = jnp.stack(parts).reshape(local_count, owners, groups, capacity, width)
        back = jnp.stack([swap(rows[:, bits], bits) for bits in range(owners)])
        sums = dot("bigct,bigck->gtk", pick_all, back).astype(BF16)
        mine = jnp.stack(
            [shift(picked(sums, my_group - step), -step) for step in range(groups)]
        )
        whole = jnp.concatenate([picked(mine, c - my_group) for c in range(groups)], axis=1)
        if sharers != 2:
            return lax.psum_scatter(whole, "tensor", scatter_dimension=1, tiled=True).astype(F32)
        half = model_width // 2
        give = lax.dynamic_slice(whole, (0, (1 - my_part) * half), (tok_count, half))
        keep = lax.dynamic_slice(whole, (0, my_part * half), (tok_count, half))
        return keep.astype(F32) + lax.ppermute(give, "tensor", [(0, 1), (1, 0)]).astype(F32)

    output = (mix * combine(part_out)).astype(BF16)
    grad_tokens = combine(part_in).astype(BF16)
    return (output, grad_tokens, jnp.stack(grad_gate), jnp.stack(grad_up), jnp.stack(grad_down))


VMEM_LIMIT = 48 * 1024 * 1024


def call(body, outs, ins, scratch=(), flops=0, specs=None):
    moved = sum(a.size * a.dtype.itemsize for a in ins)
    moved += sum(o.size * o.dtype.itemsize for o in outs)
    many = pl.BlockSpec(memory_space=pltpu.VMEM)
    return pl.pallas_call(
        body,
        out_shape=outs,
        grid=() if specs is None else (1,),
        in_specs=[many] * len(ins) if specs is None else specs,
        out_specs=[many] * len(outs),
        scratch_shapes=list(scratch),
        compiler_params=pltpu.CompilerParams(vmem_limit_bytes=VMEM_LIMIT),
        cost_estimate=pl.CostEstimate(flops=flops, bytes_accessed=moved, transcendentals=0),
    )(*ins)


def arr(shape, dtype=BF16):
    return jax.ShapeDtypeStruct(shape, dtype)


def mm(a, b):
    return jnp.dot(a, b, preferred_element_type=F32)


def mm_nt(a, b):
    return lax.dot_general(a, b, (((1,), (1,)), ((), ())), preferred_element_type=F32)


def mm_tn(a, b):
    return lax.dot_general(a, b, (((0,), (0,)), ((), ())), preferred_element_type=F32)


def kernel_form(tokens, cotangent, scores, routes, w_gate, w_up, w_down):
    toks, model_width = tokens.shape
    owners, groups = lax.axis_size("expert"), lax.axis_size("dp")
    local, width, units = w_gate.shape
    expert_count = local * owners
    cap = min(toks, 2 * toks // expert_count)
    held = local * cap
    slot_total = expert_count * cap
    pair_rows = groups // 2 * cap
    half_rows = local * owners * pair_rows
    block = owners * pair_rows
    extra = 16

    def shift(value, step):
        return lax.ppermute(value, "dp", [(j, (j + step) % groups) for j in range(groups)])

    def swap(value, bits):
        return lax.ppermute(value, "expert", [(j, j ^ bits) for j in range(owners)])

    inward, outward = [(0, 1), (3, 2)], [(1, 0), (2, 3)]

    def line_hop(value, pairs):
        return lax.ppermute(value, "dp", pairs)

    def group_at(step):
        return lax.rem(lax.axis_index("dp") + step + groups, groups)

    def columns_at(step):
        return pl.ds(pl.multiple_of(group_at(step) * width, width), width)

    def pack_body(tok_ref, route_ref, *out_refs):
        row = lax.broadcasted_iota(jnp.int32, (extra, toks), 0)
        line = jnp.broadcast_to(route_ref[...].astype(F32), (extra, toks))
        line = jnp.where(row == 0, line, 0.0).astype(BF16)
        for step in range(groups):
            out = out_refs[step]
            out[0:toks, :] = tok_ref[:, columns_at(step)]
            out[toks : toks + extra, :] = jnp.zeros((extra, width), BF16)
            out[toks : toks + extra, 0:toks] = line

    x_pack = call(
        pack_body, [arr((toks + extra, width))] * groups, [tokens, routes.reshape(1, toks)]
    )
    x_near = {step: shift(x_pack[step], step) for step in (1, 3)}

    def slots_row(line):
        first = lax.broadcasted_iota(jnp.int32, (toks, toks), 0)
        second = lax.broadcasted_iota(jnp.int32, (toks, toks), 1)
        whole = jnp.broadcast_to(line, (toks, toks))
        column = jnp.sum(jnp.where(first == second, whole, 0.0), axis=1, keepdims=True)
        same = (column == whole) & (first < second)
        place = jnp.sum(jnp.where(same, 1.0, 0.0), axis=0, keepdims=True)
        slot = (line * float(cap) + place).astype(jnp.int32)
        return slot ^ (lax.axis_index("expert") * held)

    def picker(slot):
        row = lax.broadcasted_iota(jnp.int32, (slot_total, toks), 0)
        return jnp.where(row == jnp.broadcast_to(slot, (slot_total, toks)), 1.0, 0.0).astype(BF16)

    def send_rows(pick, rows, group, out_refs, halved=False):
        sent = mm(pick, rows).astype(BF16)
        parity, place = lax.rem(group, 2), lax.div(group, 2)
        rows_at = pl.ds(pl.multiple_of(place * cap, cap), cap)
        for bits in range(owners):
            for i in range(local):
                at = bits * held + i * cap
                if halved:
                    out_refs[bits][i, rows_at, :] = sent[at : at + cap]
                else:
                    out_refs[bits][parity, i, rows_at, :] = sent[at : at + cap]

    def dispatch_x(x_ref, step, slot_ref, out_refs):
        group = group_at(-step)
        slot = slots_row(x_ref[toks : toks + extra, 0:toks][0:1].astype(F32))
        slot_ref[pl.ds(group * 8, 8), :] = jnp.broadcast_to(slot, (8, toks))
        send_rows(picker(slot), x_ref[0:toks, :], group, out_refs, halved=True)

    message = arr((2, local, pair_rows, width))
    half_message = arr((local, pair_rows, width))
    slot_rows = arr((groups * 8, toks), jnp.int32)

    def weigh_body(cot_ref, score_ref, weighted_ref, mix_ref):
        score = score_ref[...]
        mix = score[:, 0:1] / jnp.sum(score, axis=1, keepdims=True)
        mix_ref[...] = jnp.broadcast_to(mix, mix_ref.shape)
        weighted_ref[...] = (mix * cot_ref[...].astype(F32)).astype(BF16)

    weighted, mix_wide = call(
        weigh_body, [arr((toks, model_width)), arr((toks, 128), F32)], [cotangent, scores]
    )

    def other_half_body(one_ref, three_ref, kept_ref, *outs):
        send_refs, slot_ref, passed_ref = outs[:owners], outs[owners], outs[owners + 1]
        slot_ref[...] = jnp.zeros(slot_ref.shape, jnp.int32)
        dispatch_x(one_ref, 1, slot_ref, send_refs)
        dispatch_x(three_ref, 3, slot_ref, send_refs)
        passed_ref[...] = kept_ref[...]

    got = call(
        other_half_body,
        [half_message] * owners + [slot_rows, arr((toks + extra, width))],
        [x_near[1], x_near[3], x_pack[2]],
        flops=groups * slot_total * toks * width,
    )
    other_send, other_slots, x_far = got[:owners], got[owners], shift(got[owners + 1], 2)
    other_x = [other_send[0]] + [swap(other_send[bits], bits) for bits in range(1, owners)]

    def own_half_body(own_ref, far_ref, before_ref, weighted_ref, _, *outs):
        send_refs, slot_ref, d_refs = outs[:owners], outs[owners], outs[owners + 1 :]
        slot_ref[...] = before_ref[...]
        dispatch_x(own_ref, 0, slot_ref, send_refs)
        dispatch_x(far_ref, 2, slot_ref, send_refs)
        for step in range(groups):
            d_refs[step][...] = weighted_ref[:, columns_at(step)]

    got = call(
        own_half_body,
        [half_message] * owners + [slot_rows] + [arr((toks, width))] * groups,
        [x_pack[0], x_far, other_slots, weighted, other_x[1]],
        flops=groups * slot_total * toks * width,
    )
    own_send, slots, d_pack = got[:owners], got[owners], got[owners + 1 :]
    own_x = [own_send[0]] + [swap(own_send[bits], bits) for bits in range(1, owners)]
    d_got = [d_pack[0]] + [shift(d_pack[step], step) for step in range(1, groups)]

    full = pl.BlockSpec(memory_space=pltpu.VMEM)
    piece = arr((block, units))
    piece_flops = 2 * block * units * width
    dispatch_flops = 2 * groups * slot_total * toks * width
    packed = arr((2, local, block, width))

    def pack_rows(out_ref, refs):
        for half in range(2):
            for i in range(local):
                for bits in range(owners):
                    at = slice(bits * pair_rows, (bits + 1) * pair_rows)
                    out_ref[half, i, at, :] = refs[bits][half, i]

    halves, experts = range(2), range(local)
    order = [(kind, half, i) for half in halves for i in experts for kind in "gu"]
    order += [("b", half, i) for half in halves for i in experts]
    weight_of = {"g": w_gate, "u": w_up, "b": w_down}
    part, pair, total, final, near, far = {}, {}, {}, {}, {}, {}

    def first_body(*refs):
        own_refs, other_refs, rest = refs[:owners], refs[owners : 2 * owners], refs[2 * owners :]
        w_refs, d_refs, outs = rest[:2], rest[2:4], rest[4:]
        outs[3][...], outs[4][...] = d_refs[0][...], d_refs[1][...]
        parity = lax.rem(lax.axis_index("dp"), 2)
        for half, half_refs in ((parity, own_refs), (1 - parity, other_refs)):
            for i in experts:
                for bits in range(owners):
                    at = slice(bits * pair_rows, (bits + 1) * pair_rows)
                    outs[2][half, i, at, :] = half_refs[bits][i]
        for out, w_ref in zip(outs[:2], w_refs):
            out[...] = mm(outs[2][0, 0], w_ref[0]).astype(BF16)

    part[0], part[1], packed_x, d_got[1], d_got[3] = call(
        first_body,
        [piece, piece, packed] + [arr((toks, width))] * 2,
        [*own_x, *other_x, w_gate, w_up, d_got[1], d_got[3]],
        flops=2 * piece_flops,
    )
    near[0], near[1] = line_hop(part[0], inward), line_hop(part[1], inward)

    def dispatch_d_body(*refs):
        d_refs, slot_ref, out_refs = refs[:groups], refs[groups], refs[groups + 1 :]
        for step in range(groups):
            group = group_at(-step)
            slot = slot_ref[pl.ds(group * 8, 8), :][0:1]
            send_rows(picker(slot), d_refs[step][...], group, out_refs)

    def at_end():
        place = lax.axis_index("dp")
        return (place == 0) | (place == groups - 1)

    def plus(left_ref, right_ref):
        return (left_ref[...].astype(F32) + right_ref[...].astype(F32)).astype(BF16)

    count = len(order)

    def slot_call(t, rows=None, unpacked=None, also=None):
        take, cross, done = t < count, 0 <= t - 2 < count, 0 <= t - 4 < count
        ahead = t + 2 < count
        ins, specs, outs = [near[t]], [full], []
        if take:
            ins.append(part[t])
            outs.append(piece)
        if cross:
            ins += [pair[t - 2], far[t - 2]]
            outs.append(piece)
        if done:
            ins.append(total[t - 4])
            outs.append(piece)
        specs = [full] * len(ins)
        if ahead:
            kind, half, i = order[t + 2]
            ins += [rows, weight_of[kind]]
            specs += [
                pl.BlockSpec((1, 1, block, width), lambda *_: (half, i, 0, 0)),
                pl.BlockSpec((1, *weight_of[kind].shape[1:]), lambda *_: (i, 0, 0)),
            ]
            outs.append(piece)
        if ahead and cross:
            outs.append(piece)
        if unpacked is not None:
            ins += unpacked
            specs += [full] * owners
            outs.append(packed)
        if also is not None:
            ins += also[1]
            specs += [full] * len(also[1])
            outs += also[2]
        ins_count = len(ins)

        def body(*refs):
            left, right = list(refs[:ins_count]), list(refs[ins_count:])
            got_ref = left.pop(0)
            total_ref = None
            if take:
                right.pop(0)[...] = plus(left.pop(0), got_ref)
            if cross:
                total_ref = right.pop(0)
                total_ref[...] = plus(left.pop(0), left.pop(0))
            if done:
                final_ref = right.pop(0)
                final_ref[...] = jnp.where(at_end(), got_ref[...], left.pop(0)[...])
            if ahead:
                rows_ref, w_ref, part_ref = left.pop(0), left.pop(0), right.pop(0)
                product = mm_nt if kind == "b" else mm
                part_ref[...] = product(rows_ref[0, 0], w_ref[0]).astype(BF16)
                if cross:
                    right.pop(0)[...] = jnp.where(at_end(), part_ref[...], total_ref[...])
            if unpacked is not None:
                pack_rows(right.pop(0), left)
            if also is not None:
                also[0](*left, *right, *([total_ref, final_ref] if done else []))

        got = list(call(body, outs, ins, specs=specs, flops=piece_flops if ahead else 0))
        if take:
            pair[t] = got.pop(0)
            far[t] = line_hop(pair[t], [(1, 2), (2, 1)])
        if cross:
            total[t - 2] = got.pop(0)
        if done:
            final[order[t - 4]] = got.pop(0)
        if ahead:
            part[t + 2] = got.pop(0)
        if ahead and cross:
            near[t + 2] = line_hop(got.pop(0), inward + outward)
        elif ahead:
            near[t + 2] = line_hop(part[t + 2], inward)
        return got

    d_send = slot_call(
        0, packed_x, also=(dispatch_d_body, [*d_got, slots], [message] * owners)
    )
    rows_d = [d_send[0]] + [swap(d_send[bits], bits) for bits in range(1, owners)]
    for t in range(1, 5):
        slot_call(t, packed_x)
    (packed_d,) = slot_call(5, packed_x, unpacked=rows_d)
    for t in range(6, count - 1):
        slot_call(t, packed_d)

    def spread(refs, half, i, value):
        for bits in range(owners):
            rows = value[bits * pair_rows : (bits + 1) * pair_rows]
            if half is None:
                refs[bits][i] = rows
            else:
                refs[bits][half, i] = rows

    assert local == 2
    acts, two_pieces = arr((half_rows, units)), arr((2, block, units))

    last_done = order[4 * local - 1]

    def out_body(*refs):
        w_ref, outs = refs[4 * local - 1], refs[4 * local + 1 :]
        hidden_refs, (give_ref, keep_ref), (two_ref, total_ref, final_ref) = (
            outs[:2],
            outs[2:-3],
            outs[-3:],
        )
        mine = lax.axis_index("tensor")
        two_ref[0], two_ref[1] = refs[4 * local][...], total_ref[...]
        pieces = [*refs[: 4 * local - 1], final_ref]
        for half in halves:
            for i in experts:
                at = 2 * (half * local + i)
                gate, up = pieces[at][...].astype(F32), pieces[at + 1][...].astype(F32)
                rows = (gate * jax.nn.sigmoid(gate) * up).astype(BF16)
                hidden_refs[half][i * block : (i + 1) * block, :] = rows
                result = mm(rows, w_ref[i]).astype(BF16)
                left, right = result[:, :part_cols], result[:, part_cols:]
                give_ref[half, i] = jnp.where(mine == 0, right, left)
                keep_ref[half, i] = jnp.where(mine == 0, left, right)

    part_cols = width // 2
    part_rows = arr((2, local, block, part_cols))
    assert order[count - 1 - 4] == last_done
    got = slot_call(
        count - 1,
        also=(
            out_body,
            [final[name] for name in order[: 4 * local - 1]] + [w_down, total[count - 4]],
            [acts, acts] + [part_rows] * 2 + [two_pieces],
        ),
    )
    hidden, out_send, even_total = got[:2], got[2:-1], got[-1]
    even_back = line_hop(even_total, outward)
    part_message = arr((2, local, pair_rows, part_cols))

    def across(value):
        return lax.ppermute(value, "tensor", [(0, 1), (1, 0)])

    def part_body(keep_ref, got_ref, *out_refs):
        for half in halves:
            for i in experts:
                for bits in range(owners):
                    at = slice(bits * pair_rows, (bits + 1) * pair_rows)
                    out_refs[bits][half, i] = (
                        keep_ref[half, i, at, :].astype(F32) + got_ref[half, i, at, :].astype(F32)
                    ).astype(BF16)

    out_sum = call(part_body, [part_message] * owners, [out_send[1], across(out_send[0])])
    out_got = [out_sum[0]] + [swap(out_sum[bits], bits) for bits in range(1, owners)]

    def cross_body(*refs):
        for n in range(2):
            refs[4][n] = plus(refs[2 * n], refs[2 * n + 1])

    (odd_total,) = call(
        cross_body,
        [two_pieces],
        [pair[count - 2], far[count - 2], pair[count - 1], far[count - 1]],
    )
    odd_back = line_hop(odd_total, outward)

    def combined(slot_ref, group, block_of):
        place = group // 2 * cap
        rows = [
            block_of(bits, i, slice(place, place + cap))
            for bits in range(owners)
            for i in range(local)
        ]
        pick = picker(slot_ref[group * 8 : group * 8 + 1, :])
        return mm_tn(pick, jnp.concatenate(rows, axis=0)).astype(BF16)

    def into_rows(refs, grad_refs, gate_w, up_w, act_refs, in_refs):
        for i in experts:
            gate, up = refs[2 * i][...].astype(F32), refs[2 * i + 1][...].astype(F32)
            grad = jnp.where(at_end(), grad_refs[1][i], grad_refs[0][i]).astype(F32)
            rows = slice(i * block, (i + 1) * block)
            sigma = jax.nn.sigmoid(gate)
            act_gate = (grad * up * sigma * (1.0 + gate * (1.0 - sigma))).astype(BF16)
            act_up = (grad * (gate * sigma)).astype(BF16)
            act_refs[0][rows, :] = act_gate
            act_refs[1][rows, :] = act_up
            into = mm_nt(act_gate, gate_w[i]) + mm_nt(act_up, up_w[i])
            spread(in_refs, None, i, into.astype(BF16))

    def gate_up(half):
        return [final[kind, half, i] for i in experts for kind in "gu"]

    def in_even_body(*refs):
        left = list(refs)

        def several(n):
            taken = left[:n]
            del left[:n]
            return taken

        gu_refs, grad_refs, w_refs = several(2 * local), several(2), several(2)
        o_refs, (slot_ref,) = several(owners), several(1)
        act_refs, in_refs, tok_refs, (sum_ref,) = *(several(n) for n in (2, owners, groups)), left
        into_rows(gu_refs, grad_refs, *w_refs, act_refs, in_refs)
        for group in range(groups):
            sum_ref[group] = combined(
                slot_ref, group, lambda bits, i, rows: o_refs[bits][group % 2, i, rows, :]
            )
        for step in range(groups):
            tok_refs[step][...] = sum_ref[group_at(-step)]

    got = call(
        in_even_body,
        [acts, acts] + [half_message] * owners + [arr((toks, part_cols))] * groups,
        [*gate_up(0), even_total, even_back, w_gate, w_up, *out_got, slots],
        scratch=[pltpu.VMEM((groups, toks, part_cols), BF16)],
        flops=4 * local * piece_flops + dispatch_flops,
    )
    acts0, out_tok = got[:2], got[2 + owners :]
    in_got0 = [got[2]] + [swap(got[2 + bits], bits) for bits in range(1, owners)]
    out_chunk = [out_tok[0]] + [shift(out_tok[step], -step) for step in range(1, groups)]

    def last_body(*refs):
        left = list(refs)

        def several(n):
            taken = left[:n]
            del left[:n]
            return taken

        gu_refs, grad_refs = several(2 * local), several(2)
        (gate_w, up_w), _ = several(2), several(1)
        act_refs, in_refs = several(2), several(owners)
        into_rows(gu_refs, grad_refs, gate_w, up_w, act_refs, in_refs)

    got = call(
        last_body,
        [acts, acts] + [half_message] * owners,
        [
            *gate_up(1),
            *(odd_total, odd_back, w_gate, w_up),
            in_got0[1],
        ],
        flops=4 * local * piece_flops,
    )
    acts1 = got[:2]
    in_got1 = [got[2]] + [swap(got[2 + bits], bits) for bits in range(1, owners)]

    per_part = groups // 2
    part_width = per_part * width

    def assemble(chunk_refs, give_ref, keep_ref, whole_ref):
        cols = chunk_refs[0].shape[1]
        for step in range(groups):
            whole_ref[group_at(step)] = chunk_refs[step][...]
        mine = lax.axis_index("tensor")
        for j in range(per_part):
            at = slice(j * cols, (j + 1) * cols)
            give_ref[:, at] = whole_ref[(1 - mine) * per_part + j]
            keep_ref[:, at] = whole_ref[mine * per_part + j]

    def in_tokens_body(*refs):
        left = list(refs)

        def several(n):
            taken = left[:n]
            del left[:n]
            return taken

        even_refs, odd_refs, chunk_refs = several(owners), several(owners), several(groups)
        (slot_ref,), tok_refs, (give_ref, keep_ref, sum_ref, part_ref) = several(1), several(groups), left
        for group in range(groups):
            i_refs = odd_refs if group % 2 else even_refs
            sum_ref[group] = combined(
                slot_ref, group, lambda bits, i, rows: i_refs[bits][i, rows, :]
            )
        for step in range(groups):
            tok_refs[step][...] = sum_ref[group_at(-step)]
        assemble(chunk_refs, give_ref, keep_ref, part_ref)

    swapped = [arr((toks, part_width))] * 2
    whole_rows = [pltpu.VMEM((groups, toks, width), BF16)]
    got = call(
        in_tokens_body,
        [arr((toks, width))] * groups + [arr((toks, per_part * part_cols))] * 2,
        [*in_got0, *in_got1, *out_chunk, slots],
        scratch=whole_rows + [pltpu.VMEM((groups, toks, part_cols), BF16)],
        flops=dispatch_flops,
    )
    in_tok, give_out, keep_out = got[:groups], *got[groups:]
    in_chunk = [in_tok[0]] + [shift(in_tok[step], -step) for step in range(1, groups)]

    def assemble_body(*refs):
        assemble(refs[:groups], *refs[groups:])

    give_in, keep_in = call(assemble_body, swapped, in_chunk, scratch=whole_rows)

    grad_tokens = (keep_in.astype(F32) + across(give_in).astype(F32)).astype(BF16)

    def output_body(mix_ref, keep_ref, other_ref, out_ref):
        mine = lax.axis_index("tensor")
        mix = mix_ref[:, 0:1]
        for j in range(per_part):
            at = slice(j * part_cols, (j + 1) * part_cols)
            for part, ref in ((mine, keep_ref), (1 - mine, other_ref)):
                start = pl.multiple_of(j * width + part * part_cols, part_cols)
                out_ref[:, pl.ds(start, part_cols)] = (mix * ref[:, at].astype(F32)).astype(BF16)

    (output,) = call(
        output_body, [arr((toks, part_width))], [mix_wide, keep_out, across(give_out)]
    )

    def weight_grad(rows, acts, shape, rows_first):
        def body(*refs):
            for i in range(local):
                part_sum = None
                for half in range(2):
                    left, right = refs[0][half, i], refs[1 + half][i * block : (i + 1) * block, :]
                    if not rows_first:
                        left, right = right, left
                    term = mm_tn(left, right)
                    part_sum = term if part_sum is None else part_sum + term
                refs[-1][i] = part_sum

        return call(body, [arr(shape, F32)], [rows, *acts], flops=4 * piece_flops)[0]

    grad_gate = weight_grad(packed_x, [acts0[0], acts1[0]], w_gate.shape, True)
    grad_up = weight_grad(packed_x, [acts0[1], acts1[1]], w_up.shape, True)
    grad_down = weight_grad(packed_d, hidden, w_down.shape, False)
    return (output, grad_tokens, grad_gate, grad_up, grad_down)


def on_device(tokens, cotangent, scores, routes, w_gate, w_up, w_down):
    owners = lax.axis_size("expert")
    toks = tokens.shape[0]
    cap = min(toks, 2 * toks // (w_gate.shape[0] * owners))
    held = w_gate.shape[0] * cap
    fits = (
        lax.axis_size("dp") == 4
        and lax.axis_size("tensor") == 2
        and owners == 4
        and cap % 16 == 0
        and held & (held - 1) == 0
        and toks == 128
        and w_gate.shape[1] % 128 == 0
        and w_gate.shape[2] % 128 == 0
    )
    form = kernel_form if fits else plain_form
    return form(tokens, cotangent, scores, routes, w_gate, w_up, w_down)


def solution(mesh):
    in_specs = (
        P(("dp", "expert"), None),
        P(("dp", "expert"), None),
        P(("dp", "expert"), None),
        P(("dp", "expert"), None),
        P("expert", "dp", "tensor"),
        P("expert", "dp", "tensor"),
        P("expert", "tensor", "dp"),
    )
    out_specs = (
        P(("dp", "expert"), "tensor"),
        P(("dp", "expert"), "tensor"),
        P("expert", "dp", "tensor"),
        P("expert", "dp", "tensor"),
        P("expert", "tensor", "dp"),
    )
    return jax.shard_map(
        on_device, mesh=mesh, in_specs=in_specs, out_specs=out_specs, check_vma=False
    )
```
